128 devices in a mesh: sub: 32 (over y_lo, z, x), lev: 4 (over y_hi, core).
Axes of the slice: x: 4, y: 4 (y_hi: 2, y_lo: 2; y = y_hi * 2 + y_lo), z: 4, core: 2. Of those that a mesh axis runs over, the one named last changes fastest.
Arguments:
- wind_u: float32 [16, 8192, 256], P('lev', 'sub'), may hold values from -6 to 6
- wind_v: float32 [16, 8192, 256], P('lev', 'sub'), may hold values from -6 to 6
- vertical: float32 [16, 8192, 256], P('lev', 'sub'), may hold values from -6 to 6
- spacing_x: float32 [8192, 256], P('sub'), may hold values from 0.5 to 2
- spacing_y: float32 [8192, 256], P('sub'), may hold values from 0.5 to 2
- coriolis: float32 [8192, 256], P('sub'), may hold values from -4 to 4
- edge_source: int32 [32, 4], P('sub'), may hold values from 0 to 127
- edge_turns: int32 [32, 4], P('sub'), may hold values from 0 to 3
- route_owner: int32 [16384, 2], P('sub'), may hold values from 0 to 31, all different within a row; in each aligned block of 512 rows (0 to 511, 512 to 1023, ...) at most 64 rows name the same one
- route_window: int32 [16384, 2], P('sub'), may hold values from 0 to 3
- remap_weights: bfloat16 [16384, 2, 128, 128], P('sub'), may hold values from 0 to 6.1035156e-05
Outputs:
- tendencies: float32 [2, 16, 8192, 256], P(None, 'lev', 'sub')
- remapped: float32 [2, 16, 16384], P(None, 'lev', 'sub')
The draws below stay inside these ranges and needn't reach their ends.
Inputs may be any that keep to these rules, and one draw needn't show every extreme that they name: `route_owner`: each row names two different owners; among the rows of one subdomain at most 64 name one owner, a bound that some block reaches.
All inputs are finite; a program needn't handle non-finite values.
Results may differ from the reference program's by a relative error of at most 0.0031.
Values sent between devices are 32-bit elements; how exact they have to be, the bound alone decides.
No kernel may reach another device: no remote copies, remote signals or barrier semaphores. Data moves between devices by JAX's collectives and lax.ppermute only.
A program may use at most 128 MiB of HBM per device.

```python
import math
import jax
import jax.numpy as jnp
import numpy as np
from jax import lax

CS = 256
WINDOWS = 4
LEVELS = 16
BLOCKS = 512
CAP = 64
ROWS = 8192
LATLON = 16384
N_SUB = 32


def set_ends(values, rng, least, largest):
    longest = values.shape.index(max(values.shape))
    spots = []
    for shift in (0, 1):
        where = [jax.random.randint(jax.random.fold_in(rng, axis), (), 0, length) for axis, length in enumerate(values.shape)]
        where[longest] = (where[longest] + shift) % values.shape[longest]
        spots.append(tuple(where))
    return values.at[spots[0]].set(least).at[spots[1]].set(largest)


def shard_levels(key, dims, cuts, least, high):
    gain, own = 1.0, jax.random.fold_in(key, 6)
    for dim, blocks in cuts:
        heights = jnp.exp(jax.random.uniform(jax.random.fold_in(own, dim), (blocks,), jnp.float32, least / len(cuts), high / len(cuts)))
        gain = gain * jnp.repeat(heights, dims[dim] // blocks).reshape([-1 if axis == dim else 1 for axis in range(len(dims))])
    return gain


def assign_block(own_key, own, number, rows, count, top, reach, lean):
    sequence = jax.random.permutation(own_key, count)
    heavy_load, ordinary = portions_of(count, rows * top, reach, lean, True), portions_of(count, rows * top, reach, lean, False)
    places = jnp.arange(count)

    def named(sizes, turn):
        used = int((sizes > 0).sum())
        fixed = max(1, used // 4)
        passed = fixed + (places - fixed + turn * (used - fixed)) % max(1, count - fixed)
        return jnp.zeros((count,), jnp.int32).at[sequence[jnp.where(places < fixed, places, passed)]].set(jnp.asarray(sizes, jnp.int32))

    sizes = jnp.where(number % 4 == 0, named(heavy_load, number // 4), named(ordinary, number - number // 4 - 1))
    mixed = jax.random.permutation(jax.random.fold_in(own, 3), count)
    giver, taker = mixed[0:count // 2 * 2:2], mixed[1:count // 2 * 2:2]
    margin = jnp.minimum(sizes[giver] - 1, reach - sizes[taker]) // 2
    margin = jnp.where((giver == sequence[0]) | (taker == sequence[0]) | (sizes[taker] == 0), 0, jnp.maximum(margin, 0))
    passed = jax.random.randint(jax.random.fold_in(own, 4), (count // 2,), 0, 1 << 20) % (margin + 1)
    sizes = sizes.at[giver].add(-passed).at[taker].add(passed)
    labels = jnp.searchsorted(jnp.cumsum(sizes), jnp.arange(rows * top), side="right").astype(jnp.int32)
    table = labels.reshape(top, rows).T
    table = table[jax.random.permutation(jax.random.fold_in(own, 1), rows)]
    turn = jax.random.randint(jax.random.fold_in(own, 2), (rows, 1), 0, top)
    return jnp.take_along_axis(table, (jnp.arange(top)[None, :] + turn) % top, axis=1)


def portions_of(count, total, bound, lean, full):
    loads = [(1 << 20) // math.isqrt(grade ** lean) + 1 for grade in range(1, count + 1)]
    largest = bound if full else min(bound, max(-(-total // count), total * loads[0] // sum(loads)))
    least = 1 if total - largest >= count - 1 else 0
    given, spare = [largest] + [least] * (count - 1), total - largest - least * (count - 1)
    while spare > 0:
        free = [i for i in range(1, count) if given[i] < largest] or [i for i in range(1, count) if given[i] < bound]
        pool, remaining = sum([loads[i] for i in free]), spare
        for i in free:
            more = min(bound - given[i], max(1, remaining * loads[i] // pool), spare)
            given[i] = given[i] + more
            spare = spare - more
    return np.array(given)


def normal_values(key, shape, width, most, shards=(), held_as=jnp.bfloat16):
    loudness = shard_levels(key, shape, shards, -0.22, 0.18) if shards else 1.0
    values = jax.random.normal(key, shape, jnp.float32) * width * loudness
    return jnp.minimum(jnp.maximum(values, -most), most).astype(held_as)


def setup_inputs(seed: int = 0) -> dict:
    key_of = jax.random.split(jax.random.key(seed), 12)
    wind_u = normal_values(key_of[0], (LEVELS, ROWS, CS), 1.0, 6.0, ((0, 4), (1, 32)), jnp.float32)
    wind_v = normal_values(key_of[1], (LEVELS, ROWS, CS), 1.0, 6.0, ((0, 4), (1, 32)), jnp.float32)
    vertical = normal_values(key_of[2], (LEVELS, ROWS, CS), 1.0, 6.0, ((0, 4), (1, 32)), jnp.float32)
    spacing_x = jnp.clip(jnp.exp(math.log(2.0) - 1.3862944 * jax.random.uniform(key_of[3], (ROWS, CS), jnp.float32) ** shard_levels(key_of[3], (ROWS, CS), ((0, 32),), -0.2, 0.2)), 0.5, 2.0)
    spacing_y = jnp.clip(jnp.exp(math.log(2.0) - 1.3862944 * jax.random.uniform(key_of[4], (ROWS, CS), jnp.float32) ** shard_levels(key_of[4], (ROWS, CS), ((0, 32),), -0.2, 0.2)), 0.5, 2.0)
    coriolis = normal_values(key_of[5], (ROWS, CS), 1.0, 4.0, ((0, 32),), jnp.float32)
    edge_source = set_ends(jax.random.randint(key_of[6], (N_SUB, 4), 0, 4 * N_SUB), jax.random.fold_in(key_of[6], 1), 0, (4 * N_SUB) - 1).astype(jnp.int32)
    edge_turns = set_ends(jax.random.randint(key_of[7], (N_SUB, 4), 0, 4), jax.random.fold_in(key_of[7], 1), 0, 3).astype(jnp.int32)
    route_owner_keys = jax.random.split(jax.random.fold_in(key_of[8], 1), (N_SUB * BLOCKS) // BLOCKS)
    route_owner_turns = jax.random.permutation(jax.random.fold_in(key_of[8], 3), (N_SUB * BLOCKS) // BLOCKS)
    route_owner = jax.vmap(lambda own, number: assign_block(jax.random.fold_in(key_of[8], 2), own, number, BLOCKS, N_SUB, 2, CAP, 2))(route_owner_keys, route_owner_turns).reshape((N_SUB * BLOCKS, 2))
    route_window = set_ends(jax.random.randint(key_of[9], (N_SUB * BLOCKS, 2), 0, WINDOWS), jax.random.fold_in(key_of[9], 1), 0, WINDOWS - 1).astype(jnp.int32)
    remap_weights = jnp.clip(6.103515625e-05 * jax.random.uniform(key_of[10], (N_SUB * BLOCKS, 2, 128, 128), jnp.float32) ** shard_levels(key_of[10], (N_SUB * BLOCKS, 2, 128, 128), ((0, 32),), -0.2, 0.2), 0.0, 6.103515625e-05).astype(jnp.bfloat16)
    return dict(wind_u=wind_u, wind_v=wind_v, vertical=vertical, spacing_x=spacing_x, spacing_y=spacing_y, coriolis=coriolis, edge_source=edge_source, edge_turns=edge_turns, route_owner=route_owner, route_window=route_window, remap_weights=remap_weights)


def side_rows(field):
    return jnp.stack([field[..., :, 0], field[..., :, -1], field[..., 0, :], field[..., -1, :]], axis=2)


def turn_edges(edge_u, edge_v, turns):
    cosine = (turns == 0).astype(jnp.float32) - (turns == 2).astype(jnp.float32)
    sine = (turns == 1).astype(jnp.float32) - (turns == 3).astype(jnp.float32)
    new_u = cosine * edge_u - sine * edge_v
    new_v = sine * edge_u + cosine * edge_v
    odd = (turns % 2) == 1
    return jnp.where(odd, new_u[..., ::-1], new_u), jnp.where(odd, new_v[..., ::-1], new_v)


def fill_halo(field, halo):
    padded = jnp.pad(field, ((0, 0), (0, 0), (1, 1), (1, 1)))
    padded = padded.at[:, :, 1:-1, 0].set(halo[:, 0].transpose(1, 0, 2))
    padded = padded.at[:, :, 1:-1, -1].set(halo[:, 1].transpose(1, 0, 2))
    padded = padded.at[:, :, 0, 1:-1].set(halo[:, 2].transpose(1, 0, 2))
    padded = padded.at[:, :, -1, 1:-1].set(halo[:, 3].transpose(1, 0, 2))
    return padded


def reference(wind_u, wind_v, vertical, spacing_x, spacing_y, coriolis, edge_source, edge_turns, route_owner, route_window, remap_weights):
    field_u = wind_u.reshape(LEVELS, N_SUB, CS, CS)
    field_v = wind_v.reshape(LEVELS, N_SUB, CS, CS)
    lift = vertical.reshape(LEVELS, N_SUB, CS, CS)
    step_x = spacing_x.reshape(N_SUB, CS, CS)
    step_y = spacing_y.reshape(N_SUB, CS, CS)
    rotation = coriolis.reshape(N_SUB, CS, CS)
    edges_u = side_rows(field_u).transpose(1, 2, 0, 3).reshape(N_SUB * 4, LEVELS, CS)
    edges_v = side_rows(field_v).transpose(1, 2, 0, 3).reshape(N_SUB * 4, LEVELS, CS)
    halo_u, halo_v = turn_edges(edges_u[edge_source], edges_v[edge_source], edge_turns[:, :, None, None])
    padded_u = fill_halo(field_u, halo_u)
    padded_v = fill_halo(field_v, halo_v)
    kinetic = 0.5 * (padded_u * padded_u + padded_v * padded_v)
    vorticity = (padded_v[:, :, 1:-1, 2:] - padded_v[:, :, 1:-1, :-2]) / (2.0 * step_x) - (padded_u[:, :, 2:, 1:-1] - padded_u[:, :, :-2, 1:-1]) / (2.0 * step_y) + rotation
    stack_u = jnp.pad(field_u, ((1, 1), (0, 0), (0, 0), (0, 0)))
    stack_v = jnp.pad(field_v, ((1, 1), (0, 0), (0, 0), (0, 0)))
    tend_u = vorticity * field_v - (kinetic[:, :, 1:-1, 2:] - kinetic[:, :, 1:-1, :-2]) / (2.0 * step_x) - lift * (stack_u[2:] - stack_u[:-2]) * 0.5
    tend_v = -vorticity * field_u - (kinetic[:, :, 2:, 1:-1] - kinetic[:, :, :-2, 1:-1]) / (2.0 * step_y) - lift * (stack_v[2:] - stack_v[:-2]) * 0.5
    tendencies = jnp.stack([tend_u, tend_v], 0)
    blocks = tendencies.astype(jnp.bfloat16).reshape(2, LEVELS, N_SUB, BLOCKS, 128)
    blocks = blocks.transpose(2, 3, 0, 1, 4).reshape(N_SUB * BLOCKS, 2 * LEVELS, 128).astype(jnp.float32)
    weights = remap_weights.astype(jnp.float32)
    partial_value = jnp.einsum("brq,btqp->btrp", blocks, weights, precision=lax.Precision.HIGHEST)
    weight_sum = jnp.sum(weights, axis=2)
    target = (route_owner * WINDOWS + route_window).reshape(-1)
    accumulated = jnp.zeros((N_SUB * WINDOWS, 2 * LEVELS, 128), jnp.float32).at[target].add(partial_value.reshape(-1, 2 * LEVELS, 128))
    fraction = jnp.zeros((N_SUB * WINDOWS, 128), jnp.float32).at[target].add(weight_sum.reshape(-1, 128))
    result = accumulated / jnp.maximum(fraction, 1.0)[:, None, :]
    result = result.reshape(N_SUB, WINDOWS, 2, LEVELS, 128).transpose(2, 3, 0, 1, 4).reshape(2, LEVELS, LATLON)
    return tendencies.reshape(2, LEVELS, ROWS, CS), result
```

```python
import jax
import jax.numpy as jnp
from jax import lax
from jax.experimental import pallas as pl
from jax.experimental.pallas import tpu as pltpu
from jax.sharding import PartitionSpec as P

WINDOWS = 4
CS = 256
LANES = 128
CHUNK = 16
ACCS = 4
GROUP = 32
AHEAD = 4
F32 = jnp.float32
BF16 = jnp.bfloat16


def vmem():
    return pl.BlockSpec(memory_space=pltpu.VMEM)


def smem():
    return pl.BlockSpec(memory_space=pltpu.SMEM)


def hbm():
    return pl.BlockSpec(memory_space=pltpu.HBM)


def in_hbm(x):
    return pltpu.with_memory_space_constraint(x, pltpu.HBM)


def params(mib):
    return pltpu.CompilerParams(vmem_limit_bytes=mib * 1024 * 1024)


def cost(flops, size):
    return pl.CostEstimate(flops=flops, bytes_accessed=size, transcendentals=0)


def level_kernel(wind_u, wind_v, up_ref, down_ref, token_ref, held, in_sems, out_sems):
    loads, sends = [], []
    for comp, wind in enumerate((wind_u, wind_v)):
        for k, (level, out) in enumerate(((3, up_ref), (0, down_ref))):
            for half in (0, 1):
                n = 4 * comp + 2 * k + half
                rows = pl.ds(half * (CS // 2), CS // 2)
                spot = held.at[n]
                loads.append(pltpu.make_async_copy(wind.at[level, rows], spot, in_sems.at[n]))
                sends.append(pltpu.make_async_copy(spot, out.at[comp, rows], out_sems.at[n]))
    for load in loads:
        load.start()
    token_ref[...] = jnp.zeros_like(token_ref)
    for load, send in zip(loads, sends):
        load.wait()
        send.start()
    for send in sends:
        send.wait()


def take_levels(wind_u, wind_v):
    return pl.pallas_call(
        level_kernel,
        out_shape=(
            pltpu.HBM((2, CS, CS), F32),
            pltpu.HBM((2, CS, CS), F32),
            jax.ShapeDtypeStruct((8, LANES), F32),
        ),
        in_specs=[hbm(), hbm()],
        out_specs=(hbm(), hbm(), vmem()),
        scratch_shapes=[
            pltpu.VMEM((8, CS // 2, CS), F32),
            pltpu.SemaphoreType.DMA((8,)),
            pltpu.SemaphoreType.DMA((8,)),
        ],
        compiler_params=params(2),
        cost_estimate=cost(1000, 2 << 20),
        name="outer_levels",
    )(in_hbm(wind_u), in_hbm(wind_v))


def edge_kernel(wind_u, wind_v, token_ref, edges_ref, own_ref, u_ref, v_ref, held, sems, out_sems):
    del token_ref
    loads = []
    for comp, (wind, ref) in enumerate(((wind_u, u_ref), (wind_v, v_ref))):
        for level in range(4):
            sem = sems.at[4 * comp + level]
            loads.append(pltpu.make_async_copy(wind.at[level], ref.at[level], sem))
    for load in loads:
        load.start()
    lane = lax.broadcasted_iota(jnp.int32, (CS, LANES), 1)
    columns = jnp.zeros((CS, LANES), F32)
    for comp, ref in enumerate((u_ref, v_ref)):
        for level in range(4):
            loads[4 * comp + level].wait()
            for side in (0, 1):
                at = 0 if side == 0 else CS - 1
                column = ref[level, :, pl.ds(at, 1)]
                columns = jnp.where(lane == side * 8 + comp * 4 + level, column, columns)
    held[0:16, :] = jnp.transpose(columns)[0:16, :]
    for comp, ref in enumerate((u_ref, v_ref)):
        held[16 + 4 * comp : 20 + 4 * comp, :] = ref[:, 0, :]
        held[24 + 4 * comp : 28 + 4 * comp, :] = ref[:, CS - 1, :]
    copies = [pltpu.make_async_copy(held, own_ref, out_sems.at[0])]
    for d in range(edges_ref.shape[0]):
        copies.append(pltpu.make_async_copy(held, edges_ref.at[d], out_sems.at[d + 1]))
    for copy in copies:
        copy.start()
    for copy in copies:
        copy.wait()


def take_edges(wind_u, wind_v, token, owners):
    return pl.pallas_call(
        edge_kernel,
        out_shape=(pltpu.HBM((owners, 32, CS), F32), pltpu.HBM((32, CS), F32)),
        in_specs=[hbm(), hbm(), vmem()],
        out_specs=(hbm(), hbm()),
        scratch_shapes=[
            pltpu.VMEM((4, CS, CS), F32),
            pltpu.VMEM((4, CS, CS), F32),
            pltpu.VMEM((32, CS), F32),
            pltpu.SemaphoreType.DMA((8,)),
            pltpu.SemaphoreType.DMA((owners + 1,)),
        ],
        compiler_params=params(4),
        cost_estimate=cost(1000, 4 << 20),
        name="edges",
    )(in_hbm(wind_u), in_hbm(wind_v), token)


def stencil_kernel(u_ref, v_ref, lift_ref, step_x_ref, step_y_ref, coriolis_ref, tend_ref, scale_ref):
    lane = lax.broadcasted_iota(jnp.int32, (CHUNK, CS), 1)
    inner_left, inner_right = lane > 0, lane < CS - 1
    chunks = CS // CHUNK

    def stencil(c, carry):
        r0 = pl.multiple_of(c * CHUNK, CHUNK)
        before = pl.multiple_of(jnp.maximum(r0 - 8, 0), 8)
        after = pl.multiple_of(jnp.minimum(r0 + CHUNK, CS - 8), 8)
        rows = pl.ds(r0, CHUNK)
        half_x = 0.5 / step_x_ref[rows, :]
        half_y = 0.5 / step_y_ref[rows, :]
        rotation = coriolis_ref[rows, :]

        def ends(ref, level):
            top = jnp.where(c == 0, 0.0, ref[level, pl.ds(before, 8), :][7:8])
            bottom = jnp.where(c == chunks - 1, 0.0, ref[level, pl.ds(after, 8), :][0:1])
            return top, bottom

        def rise(mid, top, bottom):
            return jnp.concatenate([mid[1:], bottom], axis=0) - jnp.concatenate(
                [top, mid[: CHUNK - 1]], axis=0
            )

        def across(mid):
            return jnp.where(inner_right, pltpu.roll(mid, CS - 1, 1), 0.0) - jnp.where(
                inner_left, pltpu.roll(mid, 1, 1), 0.0
            )

        def energy(a, b):
            return 0.5 * (a * a + b * b)

        for level in range(4):
            u, v = u_ref[level, rows, :], v_ref[level, rows, :]
            top_u, bottom_u = ends(u_ref, level)
            top_v, bottom_v = ends(v_ref, level)
            kinetic = energy(u, v)
            vort = across(v) * half_x - rise(u, top_u, bottom_u) * half_y + rotation
            slope_x = across(kinetic) * half_x
            slope_y = rise(kinetic, energy(top_u, top_v), energy(bottom_u, bottom_v)) * half_y
            lift = lift_ref[level, rows, :] * 0.5
            if level == 0:
                shear_u, shear_v = u_ref[1, rows, :], v_ref[1, rows, :]
            elif level == 3:
                shear_u, shear_v = -u_ref[2, rows, :], -v_ref[2, rows, :]
            else:
                shear_u = u_ref[level + 1, rows, :] - u_ref[level - 1, rows, :]
                shear_v = v_ref[level + 1, rows, :] - v_ref[level - 1, rows, :]
            tend_ref[0, level, rows, :] = vort * v - slope_x - lift * shear_u
            tend_ref[1, level, rows, :] = -vort * u - slope_y - lift * shear_v
        return carry

    lax.fori_loop(0, chunks, stencil, 0)
    side = lax.broadcasted_iota(jnp.int32, (CS, LANES), 1)
    columns = jnp.where(side == 0, step_x_ref[:, 0:1], step_x_ref[:, CS - 1 : CS])
    steps = jnp.concatenate(
        [
            jnp.transpose(columns)[0:2],
            step_y_ref[0:1, :],
            step_y_ref[CS - 1 : CS, :],
            jnp.ones((4, CS), F32),
        ],
        axis=0,
    )
    scale_ref[...] = 0.5 / steps


def inner_tendencies(*fields):
    return pl.pallas_call(
        stencil_kernel,
        out_shape=(pltpu.HBM((2, 4, CS, CS), F32), pltpu.HBM((8, CS), F32)),
        in_specs=[vmem()] * 6,
        out_specs=(vmem(), vmem()),
        compiler_params=params(10),
        cost_estimate=cost(30 << 20, 6 << 20),
        name="stencil",
    )(*fields)


def remap_kernel(
    target_ref,
    inner_hbm,
    lift_hbm,
    below_hbm,
    above_hbm,
    weights_hbm,
    tend_hbm,
    part_hbm,
    line_hbm,
    weights_ref,
    tend_ref,
    lift_ref,
    below_ref,
    above_ref,
    part_ref,
    line_ref,
    blocks,
    *rest,
):
    accs, (sems, out_sems) = rest[:ACCS], rest[ACCS:]
    block_count = weights_ref.shape[0]
    steps = block_count // GROUP
    lines = GROUP // 2

    def loads(c):
        part = pl.ds(c * GROUP, GROUP)
        rows = pl.ds(pl.multiple_of(c * lines, lines), lines)
        pairs = [
            (inner_hbm.at[:, :, rows], tend_ref.at[:, :, rows]),
            (lift_hbm.at[0, rows], lift_ref.at[0, rows]),
            (lift_hbm.at[3, rows], lift_ref.at[1, rows]),
            (below_hbm.at[:, rows], below_ref.at[:, rows]),
            (above_hbm.at[:, rows], above_ref.at[:, rows]),
            (weights_hbm.at[part], weights_ref.at[part]),
        ]
        return [
            pltpu.make_async_copy(source, dest, sems.at[k, c])
            for k, (source, dest) in enumerate(pairs)
        ]

    def tend_out(c):
        rows = pl.ds(pl.multiple_of(c * lines, lines), lines)
        return pltpu.make_async_copy(
            tend_ref.at[:, :, rows], tend_hbm.at[:, :, rows], sems.at[6, c]
        )

    for c in range(AHEAD):
        for load in loads(c):
            load.start()
    for acc in accs:
        acc[...] = jnp.zeros_like(acc)

    def levels(r0):
        rows = pl.ds(r0, 8)
        for comp in (0, 1):
            for level in range(4):
                value = tend_ref[comp, level, rows, :]
                if level == 0:
                    value = value + lift_ref[0, rows, :] * 0.5 * below_ref[comp, rows, :]
                if level == 3:
                    value = value - lift_ref[1, rows, :] * 0.5 * above_ref[comp, rows, :]
                if level in (0, 3):
                    tend_ref[comp, level, rows, :] = value
                for h in (0, 1):
                    start = r0 * 16 + 8 * h + comp * 4 + level
                    blocks[pl.ds(start, 8, stride=16), :] = value[:, LANES * h : LANES * h + LANES]

    row = lax.broadcasted_iota(jnp.int32, (8, LANES), 0)
    lane = lax.broadcasted_iota(jnp.int32, (8, LANES), 1)
    ones = jnp.where(row == 0, 1.0, 0.0)
    extra = [jnp.where((row == 1) & (lane == q), 1.0, ones) for q in (0, LANES - 1)]

    def remap(c, carry):
        for load in loads(c):
            load.wait()

        @pl.when(c + AHEAD < steps)
        def _():
            for load in loads(c + AHEAD):
                load.start()

        for k in range(lines // 8):
            levels(pl.multiple_of(c * lines + 8 * k, 8))
        tend_out(c).start()
        parts, targets = [], []
        for k in range(GROUP):
            b = c * GROUP + k
            x = blocks[pl.ds(pl.multiple_of(b * 8, 8), 8), :]
            x = jnp.concatenate([x, extra[k & 1]], axis=0).astype(BF16)
            tiles = jnp.concatenate([weights_ref[b, 0], weights_ref[b, 1]], axis=1)
            product = jnp.dot(x, tiles, preferred_element_type=F32)
            for t in (0, 1):
                half = product[:, LANES * t : LANES * t + LANES]
                parts.append(half)
                targets.append(target_ref[t, b])
                line_ref[pl.ds(t * block_count + b, 1), :] = half[9:10]
        for first in range(0, len(parts), ACCS):
            here = range(first, first + ACCS)
            olds = [accs[i - first][targets[i]] for i in here]
            for i, old in zip(here, olds):
                accs[i - first][targets[i]] = old + parts[i]
        return carry

    lax.fori_loop(0, steps, remap, 0)
    line_out = pltpu.make_async_copy(line_ref, line_hbm, out_sems.at[0])
    line_out.start()

    def gather(o, carry):
        sums = []
        for w in range(WINDOWS):
            total = accs[0][o * WINDOWS + w]
            for acc in accs[1:]:
                total = total + acc[o * WINDOWS + w]
            part_ref[o, w * 8 : w * 8 + 8, :] = total[0:8]
            sums.append(total[8:9])
        part_ref[o, 32:40, :] = jnp.concatenate(sums + [jnp.zeros((4, LANES), F32)], axis=0)
        return carry

    lax.fori_loop(0, part_ref.shape[0], gather, 0)
    part_out = pltpu.make_async_copy(part_ref, part_hbm, out_sems.at[1])
    part_out.start()
    for out in (line_out, part_out):
        out.wait()

    def drain(c, carry):
        tend_out(c).wait()
        return carry

    lax.fori_loop(0, steps, drain, 0)


def remap_inner(target, inner, lift, below, above, weights, owners):
    blocks = weights.shape[0]
    return pl.pallas_call(
        remap_kernel,
        out_shape=(
            pltpu.HBM((2, 4, CS, CS), F32),
            pltpu.HBM((owners, 40, LANES), F32),
            pltpu.HBM((2 * blocks, LANES), F32),
        ),
        in_specs=[smem()] + [hbm()] * 5,
        out_specs=(hbm(), hbm(), hbm()),
        scratch_shapes=[
            pltpu.VMEM(weights.shape, BF16),
            pltpu.VMEM((2, 4, CS, CS), F32),
            pltpu.VMEM((2, CS, CS), F32),
            pltpu.VMEM((2, CS, CS), F32),
            pltpu.VMEM((2, CS, CS), F32),
            pltpu.VMEM((owners, 40, LANES), F32),
            pltpu.VMEM((2 * blocks, LANES), F32),
            pltpu.VMEM((blocks * 8, LANES), F32),
        ]
        + [pltpu.VMEM((owners * WINDOWS, 16, LANES), F32)] * ACCS
        + [
            pltpu.SemaphoreType.DMA((7, blocks // GROUP)),
            pltpu.SemaphoreType.DMA((2,)),
        ],
        compiler_params=params(48),
        cost_estimate=cost(2 * 1024 * 16 * 128 * 128, 36 << 20),
        name="remap",
    )(target, *[in_hbm(x) for x in (inner, lift, below, above, weights)])


def reverse_lanes(x):
    rows = x.shape[0]
    i = lax.broadcasted_iota(jnp.int32, (CS, CS), 0)
    j = lax.broadcasted_iota(jnp.int32, (CS, CS), 1)
    flip = jnp.where(i + j == CS - 1, 1.0, 0.0).astype(BF16)
    high = x.astype(BF16)
    rest = x - high.astype(F32)
    mid = rest.astype(BF16)
    low = (rest - mid.astype(F32)).astype(BF16)
    parts = jnp.dot(jnp.concatenate([high, mid, low], axis=0), flip, preferred_element_type=F32)
    return parts[0:rows] + parts[rows : 2 * rows] + parts[2 * rows : 3 * rows]


def fix_kernel(
    source_ref,
    turns_ref,
    target_ref,
    lanes_ref,
    own_ref,
    scale_ref,
    part_hbm,
    line_hbm,
    edges_ref,
    weights_hbm,
    send_hbm,
    delta_ref,
    got,
    ends,
    line_ref,
    send_ref,
    sems,
):
    copies = []
    for s in range(4):
        e = source_ref[0, s]
        copies.append(
            pltpu.make_async_copy(
                edges_ref.at[e >> 2, pl.ds(pl.multiple_of((e & 3) * 8, 8), 8)],
                got.at[s],
                sems.at[s],
            )
        )
    block_count = weights_hbm.shape[0]
    for k, at in enumerate((0, block_count - 2)):
        copies.append(
            pltpu.make_async_copy(
                weights_hbm.at[pl.ds(at, 2)], ends.at[pl.ds(2 * k, 2)], sems.at[4 + k]
            )
        )
    copies.append(pltpu.make_async_copy(line_hbm, line_ref, sems.at[6]))
    copies.append(pltpu.make_async_copy(part_hbm, send_ref, sems.at[7]))
    for copy in copies:
        copy.start()
    for copy in copies:
        copy.wait()

    upper = lax.broadcasted_iota(jnp.int32, (8, CS), 0) < 4
    sign = jnp.where(upper, -1.0, 1.0)
    turned = []
    for s in range(4):
        k = turns_ref[0, s]
        cosine = jnp.where(k == 0, 1.0, 0.0) - jnp.where(k == 2, 1.0, 0.0)
        sine = jnp.where(k == 1, 1.0, 0.0) - jnp.where(k == 3, 1.0, 0.0)
        edge = got[s]
        turned.append(cosine * edge + sine * (sign * pltpu.roll(edge, 4, 0)))
    flipped = reverse_lanes(jnp.concatenate(turned, axis=0))
    deltas = []
    for s in range(4):
        odd = (turns_ref[0, s] & 1) == 1
        halo = jnp.where(odd, flipped[8 * s : 8 * s + 8], turned[s])
        other = pltpu.roll(halo, 4, 0)
        energy = 0.5 * (halo * halo + other * other)
        out = -1.0 if s in (0, 3) else 1.0
        half = scale_ref[s : s + 1, :]
        if s < 2:
            vort = out * half * jnp.where(upper, other, halo)
            kinetic = jnp.where(upper, -out * half * energy, 0.0)
        else:
            vort = out * half * jnp.where(upper, halo, other)
            kinetic = jnp.where(upper, 0.0, out * half * energy)
        across = pltpu.roll(own_ref[8 * s : 8 * s + 8, :], 4, 0)
        delta = kinetic - sign * vort * across
        deltas.append(delta)
        delta_ref[s] = delta

    cell = lax.broadcasted_iota(jnp.int32, (CS, block_count), 0)
    block = lax.broadcasted_iota(jnp.int32, (CS, block_count), 1)
    values = sum(
        jnp.dot(
            deltas[s].astype(BF16),
            jnp.where(block == 2 * cell + s, 1.0, 0.0).astype(BF16),
            preferred_element_type=F32,
        )
        for s in (0, 1)
    )
    values = jnp.concatenate([values, values], axis=1)
    lines = line_ref[...].astype(BF16)
    targets = jnp.broadcast_to(lanes_ref[...], values.shape)
    owners = send_ref.shape[0]
    wide = 4
    for o in range(0, owners, wide):
        rows = [
            jnp.where(targets == w, values, 0.0)
            for w in range(o * WINDOWS, (o + wide) * WINDOWS)
        ]
        columns = jnp.dot(
            jnp.concatenate(rows, axis=0).astype(BF16), lines, preferred_element_type=F32
        )
        for k in range(wide):
            send_ref[o + k, 0:32, :] += columns[32 * k : 32 * k + 32]

    blank = jnp.zeros((8, LANES), F32)
    products = []
    for k in range(4):
        line = deltas[2 + k // 2][:, LANES * (k & 1) : LANES * (k & 1) + LANES]
        x = jnp.concatenate([line, blank], axis=0).astype(BF16)
        tiles = jnp.concatenate([ends[k, 0], ends[k, 1]], axis=1)
        products.append(jnp.dot(x, tiles, preferred_element_type=F32))
    for k, b in enumerate((0, 1, block_count - 2, block_count - 1)):
        for t in (0, 1):
            at = target_ref[t, b]
            rows = pl.ds(pl.multiple_of((at & 3) * 8, 8), 8)
            send_ref[at >> 2, rows, :] += products[k][0:8, LANES * t : LANES * t + LANES]
    out = pltpu.make_async_copy(send_ref, send_hbm, sems.at[8])
    out.start()
    out.wait()


def fix_edges(source, turns, target, lanes, own, scale, part, line, edges, weights):
    return pl.pallas_call(
        fix_kernel,
        out_shape=(pltpu.HBM(part.shape, F32), jax.ShapeDtypeStruct((4, 8, CS), F32)),
        in_specs=[smem()] * 3 + [vmem()] * 3 + [hbm()] * 4,
        out_specs=(hbm(), vmem()),
        scratch_shapes=[
            pltpu.VMEM((4, 8, CS), F32),
            pltpu.VMEM((4, 2, LANES, LANES), BF16),
            pltpu.VMEM(line.shape, F32),
            pltpu.VMEM(part.shape, F32),
            pltpu.SemaphoreType.DMA((9,)),
        ],
        compiler_params=params(10),
        cost_estimate=cost(2 * 1024 * 1024 * 128, 3 << 20),
        name="edge_fix",
    )(source, turns, target, lanes, own, scale, *[in_hbm(x) for x in (part, line, edges, weights)])


def place_kernel(tend_ref, delta_ref, out_ref, cols):
    cols[...] = jnp.transpose(
        jnp.concatenate(
            [delta_ref[0], delta_ref[1], jnp.zeros((LANES - 16, CS), F32)], axis=0
        )
    )
    lane = lax.broadcasted_iota(jnp.int32, (CS, LANES), 1)
    for comp in (0, 1):
        for level in range(4):
            r = comp * 4 + level
            left, right = cols[:, r : r + 1], cols[:, 8 + r : 9 + r]
            value = tend_ref[comp, level, :, 0:LANES]
            out_ref[comp, level, :, 0:LANES] = value + jnp.where(lane == 0, left, 0.0)
            value = tend_ref[comp, level, :, LANES:CS]
            out_ref[comp, level, :, LANES:CS] = value + jnp.where(lane == LANES - 1, right, 0.0)
            out_ref[comp, level, 0:1, :] += delta_ref[2, r : r + 1, :]
            out_ref[comp, level, CS - 1 : CS, :] += delta_ref[3, r : r + 1, :]


def place(tend, delta):
    return pl.pallas_call(
        place_kernel,
        out_shape=jax.ShapeDtypeStruct(tend.shape, F32),
        in_specs=[vmem(), vmem()],
        out_specs=vmem(),
        scratch_shapes=[pltpu.VMEM((CS, LANES), F32)],
        compiler_params=params(8),
        cost_estimate=cost(1 << 20, 4 << 20),
        name="place",
    )(tend, delta)


def finish_kernel(got_ref, out_ref):
    total = got_ref[0]
    for d in range(1, got_ref.shape[0]):
        total = total + got_ref[d]
    for w in range(WINDOWS):
        share = total[8 * w : 8 * w + 8] / jnp.maximum(total[32 + w : 33 + w], 1.0)
        out_ref[0, :, LANES * w : LANES * w + LANES] = share[0:4]
        out_ref[1, :, LANES * w : LANES * w + LANES] = share[4:8]


def finish(got):
    return pl.pallas_call(
        finish_kernel,
        out_shape=jax.ShapeDtypeStruct((2, 4, WINDOWS * LANES), F32),
        in_specs=[vmem()],
        out_specs=vmem(),
        compiler_params=params(4),
        cost_estimate=cost(1000, 1 << 20),
        name="finish",
    )(got)


def per_device(
    wind_u,
    wind_v,
    vertical,
    spacing_x,
    spacing_y,
    coriolis,
    edge_source,
    edge_turns,
    route_owner,
    route_window,
    remap_weights,
):
    owners = lax.axis_size("sub")
    groups = lax.axis_size("lev")
    top, bottom, token = take_levels(wind_u, wind_v)
    edges, own = take_edges(wind_u, wind_v, token, owners)
    below = lax.ppermute(top, "lev", [(i, i + 1) for i in range(groups - 1)])
    above = lax.ppermute(bottom, "lev", [(i + 1, i) for i in range(groups - 1)])
    edges = lax.all_to_all(edges, "sub", split_axis=0, concat_axis=0, tiled=True)
    target = (route_owner * WINDOWS + route_window).T
    lanes = target.reshape(1, target.size)
    inner, scale = inner_tendencies(wind_u, wind_v, vertical, spacing_x, spacing_y, coriolis)
    tend, part, line = remap_inner(target, inner, vertical, below, above, remap_weights, owners)
    send, delta = fix_edges(
        edge_source, edge_turns, target, lanes, own, scale, part, line, edges, remap_weights
    )
    got = lax.all_to_all(send, "sub", split_axis=0, concat_axis=0, tiled=True)
    return place(tend, delta), finish(got)


def solution(mesh):
    placed = (
        P("lev", "sub", None),
        P("lev", "sub", None),
        P("lev", "sub", None),
        P("sub", None),
        P("sub", None),
        P("sub", None),
        P("sub", None),
        P("sub", None),
        P("sub", None),
        P("sub", None),
        P("sub", None, None, None),
    )
    return jax.shard_map(
        per_device,
        mesh=mesh,
        in_specs=placed,
        out_specs=(P(None, "lev", "sub", None), P(None, "lev", "sub")),
        check_vma=False,
    )
```

```python
import jax
import jax.numpy as jnp
from jax import lax
from jax.experimental import pallas as pl
from jax.experimental.pallas import tpu as pltpu
from jax.sharding import PartitionSpec as P

WINDOWS = 4
CS = 256
LANES = 128
CHUNK = 16
ACCS = 4
GROUP = 64
PIECE = 32
HELD = 128
SPLIT = CS // CHUNK // 2 - 1
QUARTERS = 4
F32 = jnp.float32
BF16 = jnp.bfloat16


def vmem():
    return pl.BlockSpec(memory_space=pltpu.VMEM)


def smem():
    return pl.BlockSpec(memory_space=pltpu.SMEM)


def anywhere():
    return pl.BlockSpec(memory_space=pl.ANY)


def hbm():
    return pl.BlockSpec(memory_space=pltpu.HBM)


def in_hbm(x):
    return pltpu.with_memory_space_constraint(x, pltpu.HBM)


def in_vmem(x):
    return pltpu.with_memory_space_constraint(x, pltpu.VMEM)


def params(mib):
    return pltpu.CompilerParams(vmem_limit_bytes=mib * 1024 * 1024)


def cost(flops, size):
    return pl.CostEstimate(flops=flops, bytes_accessed=size, transcendentals=0)


def edge_kernel(
    wind_u, wind_v, edges_ref, own_ref, far_ref, near_ref, u_ref, v_ref, held, in_sems, out_sems
):
    loads, sends = [], []
    order = [(comp, level) for level in (0, 3, 1, 2) for comp in (0, 1)]
    winds, refs = (wind_u, wind_v), (u_ref, v_ref)
    for k, (comp, level) in enumerate(order):
        loads.append(
            pltpu.make_async_copy(winds[comp].at[level], refs[comp].at[level], in_sems.at[k])
        )
    for load in loads:
        load.start()
    lane = lax.broadcasted_iota(jnp.int32, (CS, LANES), 1)
    columns = jnp.zeros((CS, LANES), F32)
    for k, (comp, level) in enumerate(order):
        loads[k].wait()
        ref = refs[comp]
        if level in (0, 3):
            if level == 3:
                odd = lax.rem(lax.axis_index("lev"), 2)
                for n, (out, at) in enumerate(((far_ref, 3 * odd), (near_ref, 3 - 3 * odd))):
                    sem = out_sems.at[2 * comp + n]
                    sends.append(pltpu.make_async_copy(ref.at[at], out.at[comp], sem))
                    sends[-1].start()
        for side in (0, 1):
            at = 0 if side == 0 else CS - 1
            column = ref[level, :, pl.ds(at, 1)]
            columns = jnp.where(lane == side * 8 + comp * 4 + level, column, columns)
    parts = [jnp.transpose(columns)[0:16, :]]
    for at in (0, CS - 1):
        for ref in refs:
            parts.append(ref[:, at, :])
    edges = jnp.concatenate(parts, axis=0)
    owners = held.shape[0]
    for d in range(owners):
        held[d] = edges
    sends.append(pltpu.make_async_copy(held.at[0], own_ref, out_sems.at[4]))
    sends[-1].start()
    for k in range(4):
        part = pl.ds(k * (owners // 4), owners // 4)
        sends.append(pltpu.make_async_copy(held.at[part], edges_ref.at[part], out_sems.at[k + 5]))
        sends[-1].start()
    for send in sends:
        send.wait()


def take_edges(wind_u, wind_v, owners):
    return pl.pallas_call(
        edge_kernel,
        out_shape=(
            pltpu.HBM((owners, 32, CS), F32),
            pltpu.HBM((32, CS), F32),
            pltpu.HBM((2, CS, CS), F32),
            pltpu.HBM((2, CS, CS), F32),
        ),
        in_specs=[hbm(), hbm()],
        out_specs=(hbm(),) * 4,
        scratch_shapes=[
            pltpu.VMEM((4, CS, CS), F32),
            pltpu.VMEM((4, CS, CS), F32),
            pltpu.VMEM((owners, 32, CS), F32),
            pltpu.SemaphoreType.DMA((8,)),
            pltpu.SemaphoreType.DMA((9,)),
        ],
        compiler_params=params(5),
        cost_estimate=cost(1000, 4 << 20),
        name="edges",
    )(in_hbm(wind_u), in_hbm(wind_v))


def spread(blocks, r0, r, value):
    for part in range(value.shape[0] // 8):
        for h in (0, 1):
            start = (r0 + part * 8) * 16 + 8 * h + r
            blocks[pl.ds(start, 8, stride=16), :] = value[
                8 * part : 8 * part + 8, LANES * h : LANES * h + LANES
            ]


def half_loads(sources, dests, sems):
    halves = []
    for h in (0, 1):
        rows = pl.ds(h * (CS // 2), CS // 2)
        copies = []
        for k, (source, dest) in enumerate(zip(sources, dests)):
            if len(source.shape) == 3:
                source, dest = source.at[:, rows], dest.at[:, rows]
            else:
                source, dest = source.at[rows], dest.at[rows]
            copies.append(pltpu.make_async_copy(source, dest, sems.at[h, k]))
        halves.append(copies)
    return halves


def stencil_step(u_ref, v_ref, lift_ref, step_x_ref, step_y_ref, coriolis_ref, put):
    lane = lax.broadcasted_iota(jnp.int32, (CHUNK, CS), 1)
    inner_left, inner_right = lane > 0, lane < CS - 1
    chunks = CS // CHUNK

    def stencil(c, carry):
        r0 = pl.multiple_of(c * CHUNK, CHUNK)
        before = pl.multiple_of(jnp.maximum(r0 - 8, 0), 8)
        after = pl.multiple_of(jnp.minimum(r0 + CHUNK, CS - 8), 8)
        rows = pl.ds(r0, CHUNK)
        half_x = 0.5 / step_x_ref[rows, :]
        half_y = 0.5 / step_y_ref[rows, :]
        rotation = coriolis_ref[rows, :]

        def ends(ref, level):
            top = jnp.where(c == 0, 0.0, ref[level, pl.ds(before, 8), :][7:8])
            bottom = jnp.where(c == chunks - 1, 0.0, ref[level, pl.ds(after, 8), :][0:1])
            return top, bottom

        def rise(mid, top, bottom):
            return jnp.concatenate([mid[1:], bottom], axis=0) - jnp.concatenate(
                [top, mid[: CHUNK - 1]], axis=0
            )

        def across(mid):
            return jnp.where(inner_right, pltpu.roll(mid, CS - 1, 1), 0.0) - jnp.where(
                inner_left, pltpu.roll(mid, 1, 1), 0.0
            )

        def energy(a, b):
            return 0.5 * (a * a + b * b)

        for level in range(4):
            u, v = u_ref[level, rows, :], v_ref[level, rows, :]
            top_u, bottom_u = ends(u_ref, level)
            top_v, bottom_v = ends(v_ref, level)
            kinetic = energy(u, v)
            vort = across(v) * half_x - rise(u, top_u, bottom_u) * half_y + rotation
            slope_x = across(kinetic) * half_x
            slope_y = rise(kinetic, energy(top_u, top_v), energy(bottom_u, bottom_v)) * half_y
            lift = lift_ref[level, rows, :] * 0.5
            if level == 0:
                shear_u, shear_v = u_ref[1, rows, :], v_ref[1, rows, :]
            elif level == 3:
                shear_u, shear_v = -u_ref[2, rows, :], -v_ref[2, rows, :]
            else:
                shear_u = u_ref[level + 1, rows, :] - u_ref[level - 1, rows, :]
                shear_v = v_ref[level + 1, rows, :] - v_ref[level - 1, rows, :]
            put(r0, level, vort * v - slope_x - lift * shear_u)
            put(r0, 4 + level, -vort * u - slope_y - lift * shear_v)
        return carry

    return stencil


def stencil_kernel(
    u_hbm,
    v_hbm,
    step_x_hbm,
    step_y_hbm,
    coriolis_hbm,
    lift_hbm,
    weights_hbm,
    blocks,
    scale_ref,
    lift_ref,
    held_ref,
    u_ref,
    v_ref,
    step_x_ref,
    step_y_ref,
    coriolis_ref,
    field_sems,
    sems,
):
    loads = half_loads(
        (u_hbm, v_hbm, step_x_hbm, step_y_hbm, coriolis_hbm, lift_hbm),
        (u_ref, v_ref, step_x_ref, step_y_ref, coriolis_ref, lift_ref),
        field_sems,
    )
    for load in loads[0] + loads[1]:
        load.start()
    copies = []
    for k in range(HELD // PIECE):
        part = pl.ds(k * PIECE, PIECE)
        copies.append(pltpu.make_async_copy(weights_hbm.at[part], held_ref.at[part], sems.at[k]))
    step = stencil_step(
        u_ref, v_ref, lift_ref, step_x_ref, step_y_ref, coriolis_ref, lambda *at: spread(blocks, *at)
    )
    for load in loads[0]:
        load.wait()
    for copy in copies:
        copy.start()
    lax.fori_loop(0, SPLIT, step, 0)
    for load in loads[1]:
        load.wait()
    lax.fori_loop(SPLIT, CS // CHUNK, step, 0)
    side = lax.broadcasted_iota(jnp.int32, (CS, LANES), 1)
    columns = jnp.where(side == 0, step_x_ref[:, 0:1], step_x_ref[:, CS - 1 : CS])
    steps = jnp.concatenate(
        [
            jnp.transpose(columns)[0:2],
            step_y_ref[0:1, :],
            step_y_ref[CS - 1 : CS, :],
            jnp.ones((4, CS), F32),
        ],
        axis=0,
    )
    scale_ref[...] = 0.5 / steps
    for copy in copies:
        copy.wait()


def inner_tendencies(fields, weights):
    return pl.pallas_call(
        stencil_kernel,
        out_shape=(
            pltpu.VMEM((CS * 16, LANES), F32),
            pltpu.HBM((8, CS), F32),
            pltpu.VMEM((4, CS, CS), F32),
            pltpu.VMEM((HELD,) + weights.shape[1:], BF16),
        ),
        in_specs=[hbm()] * 7,
        out_specs=(vmem(),) * 4,
        scratch_shapes=[
            pltpu.VMEM((4, CS, CS), F32),
            pltpu.VMEM((4, CS, CS), F32),
            pltpu.VMEM((CS, CS), F32),
            pltpu.VMEM((CS, CS), F32),
            pltpu.VMEM((CS, CS), F32),
            pltpu.SemaphoreType.DMA((2, 6)),
            pltpu.SemaphoreType.DMA((HELD // PIECE,)),
        ],
        compiler_params=params(10),
        cost_estimate=cost(0, 0),
        name="stencil",
    )(*[in_hbm(x) for x in fields], in_hbm(weights))


def outer_terms(odd, lift_ref, far_ref, near_ref):
    sides = ((far_ref, 3 * odd, odd), (near_ref, 3 - 3 * odd, 1 - odd))

    def terms(rows):
        out = []
        for ref, level, top in sides:
            lift = lift_ref[level, rows, :] * jnp.where(top == 1, -0.5, 0.5)
            out += [(comp, level, lift * ref[comp, rows, :]) for comp in (0, 1)]
        return out

    return terms


def remap_kernel(
    owner_ref,
    window_ref,
    blocks_in,
    held_ref,
    lift_ref,
    far_ref,
    near_ref,
    weights_hbm,
    part_hbm,
    line_hbm,
    far_hbm,
    near_hbm,
    part_ref,
    blocks,
    line_ref,
    rest_ref,
    *rest,
):
    accs, (sems, in_sems) = rest[:ACCS], rest[ACCS:]
    block_count = weights_hbm.shape[0]
    steps = block_count // GROUP
    held_steps = HELD // GROUP
    lines = GROUP // 2

    def load(c):
        source = weights_hbm.at[pl.ds(HELD + c * PIECE, PIECE)]
        return pltpu.make_async_copy(source, rest_ref.at[pl.ds(c * PIECE, PIECE)], sems.at[c])

    for acc in accs:
        acc[...] = jnp.zeros_like(acc)
    for c in range((block_count - HELD) // PIECE):
        load(c).start()
    outs = [
        pltpu.make_async_copy(far_ref, far_hbm, in_sems.at[3]),
        pltpu.make_async_copy(near_ref, near_hbm, in_sems.at[4]),
    ]
    for out in outs:
        out.start()
    odd = lax.rem(lax.axis_index("lev"), 2)
    terms = outer_terms(odd, lift_ref, far_ref, near_ref)

    def levels(r0):
        part = pl.ds(pl.multiple_of(r0 * 16, 128), 128)
        blocks[part, :] = blocks_in[part, :]
        for comp, level, value in terms(pl.ds(r0, 8)):
            for h in (0, 1):
                spot = pl.ds(r0 * 16 + 8 * h + comp * 4 + level, 8, stride=16)
                half = value[:, LANES * h : LANES * h + LANES]
                blocks[spot, :] = blocks_in[spot, :] + half

    row = lax.broadcasted_iota(jnp.int32, (8, LANES), 0)
    lane = lax.broadcasted_iota(jnp.int32, (8, LANES), 1)
    ones = jnp.where(row == 0, 1.0, 0.0)
    extra = [jnp.where((row == 1) & (lane == q), 1.0, ones) for q in (0, LANES - 1)]

    def remap(c, weights_ref, first_block):
        for k in range(lines // 8):
            levels(pl.multiple_of(c * lines + 8 * k, 8))
        parts, targets = [], []
        for k in range(GROUP):
            b = c * GROUP + k
            x = blocks[pl.ds(pl.multiple_of(b * 8, 8), 8), :]
            x = jnp.concatenate([x, extra[k & 1]], axis=0).astype(BF16)
            here = b - first_block
            tiles = jnp.concatenate([weights_ref[here, 0], weights_ref[here, 1]], axis=1)
            product = jnp.dot(x, tiles, preferred_element_type=F32)
            for t in (0, 1):
                half = product[:, LANES * t : LANES * t + LANES]
                parts.append(half)
                targets.append(owner_ref[t, b] * WINDOWS + window_ref[t, b])
                line_ref[pl.ds(t * block_count + b, 1), :] = half[9:10]
        for first in range(0, len(parts), ACCS):
            here = range(first, first + ACCS)
            olds = [accs[i - first][targets[i]] for i in here]
            for i, old in zip(here, olds):
                accs[i - first][targets[i]] = old + parts[i]

    def remap_held(c, carry):
        remap(c, held_ref, 0)
        return carry

    def remap_rest(c, carry):
        for k in range(GROUP // PIECE):
            load((c - held_steps) * (GROUP // PIECE) + k).wait()
        remap(c, rest_ref, HELD)
        return carry

    lax.fori_loop(0, held_steps, remap_held, 0)
    lax.fori_loop(held_steps, steps, remap_rest, 0)
    line_out = pltpu.make_async_copy(line_ref, line_hbm, in_sems.at[2])
    line_out.start()

    def gather(o, carry):
        sums = []
        for w in range(WINDOWS):
            total = accs[0][o * WINDOWS + w]
            for acc in accs[1:]:
                total = total + acc[o * WINDOWS + w]
            part_ref[o, w * 8 : w * 8 + 8, :] = total[0:8]
            sums.append(total[8:9])
        part_ref[o, 32:40, :] = jnp.concatenate(sums + [jnp.zeros((4, LANES), F32)], axis=0)
        return carry

    size = part_ref.shape[0] // QUARTERS
    for k in range(QUARTERS):
        lax.fori_loop(k * size, (k + 1) * size, gather, 0)
        spot = pl.ds(k * size, size)
        outs.append(pltpu.make_async_copy(part_ref.at[spot], part_hbm.at[spot], in_sems.at[5 + k]))
        outs[-1].start()
    for out in outs + [line_out]:
        out.wait()


def remap_inner(route, blocks, held, lift, far, near, weights, owners):
    count = weights.shape[0]
    return pl.pallas_call(
        remap_kernel,
        out_shape=(
            pltpu.HBM((owners, 40, LANES), F32),
            pltpu.HBM((2 * count, LANES), F32),
            pltpu.HBM((2, CS, CS), F32),
            pltpu.HBM((2, CS, CS), F32),
        ),
        in_specs=[smem()] * 2 + [vmem()] * 5 + [hbm()],
        out_specs=(hbm(),) * 4,
        scratch_shapes=[
            pltpu.VMEM((owners, 40, LANES), F32),
            pltpu.VMEM(blocks.shape, F32),
            pltpu.VMEM((2 * count, LANES), F32),
            pltpu.VMEM((count - HELD,) + weights.shape[1:], BF16),
        ]
        + [pltpu.VMEM((owners * WINDOWS, 16, LANES), F32)] * ACCS
        + [
            pltpu.SemaphoreType.DMA(((count - HELD) // PIECE,)),
            pltpu.SemaphoreType.DMA((5 + QUARTERS,)),
        ],
        compiler_params=params(36),
        cost_estimate=cost(10**15, 1 << 40),
        name="remap",
    )(
        *route,
        *[in_vmem(x) for x in (blocks, held, lift)],
        far,
        near,
        in_hbm(weights),
    )


def reverse_lanes(x):
    rows = x.shape[0]
    i = lax.broadcasted_iota(jnp.int32, (CS, CS), 0)
    j = lax.broadcasted_iota(jnp.int32, (CS, CS), 1)
    flip = jnp.where(i + j == CS - 1, 1.0, 0.0).astype(BF16)
    high = x.astype(BF16)
    rest = x - high.astype(F32)
    mid = rest.astype(BF16)
    low = (rest - mid.astype(F32)).astype(BF16)
    parts = jnp.dot(jnp.concatenate([high, mid, low], axis=0), flip, preferred_element_type=F32)
    return parts[0:rows] + parts[rows : 2 * rows] + parts[2 * rows : 3 * rows]


def fix_kernel(
    source_ref,
    turns_ref,
    owner_ref,
    window_ref,
    owners_ref,
    windows_ref,
    own_ref,
    scale_ref,
    edges_any,
    part_hbm,
    line_hbm,
    weights_hbm,
    send_hbm,
    delta_ref,
    got,
    ends,
    line_ref,
    send_ref,
    sems,
):
    edge_copies, copies = [], []
    for s in range(4):
        e = source_ref[0, s]
        spot = edges_any.at[e >> 2, pl.ds(pl.multiple_of((e & 3) * 8, 8), 8)]
        edge_copies.append(pltpu.make_async_copy(spot, got.at[s], sems.at[s]))
    block_count = weights_hbm.shape[0]
    for k, at in enumerate((0, block_count - 2)):
        copies.append(
            pltpu.make_async_copy(
                weights_hbm.at[pl.ds(at, 2)], ends.at[pl.ds(2 * k, 2)], sems.at[4 + k]
            )
        )
    copies.append(pltpu.make_async_copy(line_hbm, line_ref, sems.at[6]))
    copies.append(pltpu.make_async_copy(part_hbm, send_ref, sems.at[7]))
    for copy in edge_copies + copies:
        copy.start()
    for copy in edge_copies:
        copy.wait()

    upper = lax.broadcasted_iota(jnp.int32, (8, CS), 0) < 4
    sign = jnp.where(upper, -1.0, 1.0)
    turned = []
    for s in range(4):
        k = turns_ref[0, s]
        cosine = jnp.where(k == 0, 1.0, 0.0) - jnp.where(k == 2, 1.0, 0.0)
        sine = jnp.where(k == 1, 1.0, 0.0) - jnp.where(k == 3, 1.0, 0.0)
        edge = got[s]
        turned.append(cosine * edge + sine * (sign * pltpu.roll(edge, 4, 0)))
    flipped = reverse_lanes(jnp.concatenate(turned, axis=0))
    deltas = []
    for s in range(4):
        odd = (turns_ref[0, s] & 1) == 1
        halo = jnp.where(odd, flipped[8 * s : 8 * s + 8], turned[s])
        other = pltpu.roll(halo, 4, 0)
        energy = 0.5 * (halo * halo + other * other)
        out = -1.0 if s in (0, 3) else 1.0
        half = scale_ref[s : s + 1, :]
        if s < 2:
            vort = out * half * jnp.where(upper, other, halo)
            kinetic = jnp.where(upper, -out * half * energy, 0.0)
        else:
            vort = out * half * jnp.where(upper, halo, other)
            kinetic = jnp.where(upper, 0.0, out * half * energy)
        across = pltpu.roll(own_ref[8 * s : 8 * s + 8, :], 4, 0)
        delta = kinetic - sign * vort * across
        deltas.append(delta)
        delta_ref[s] = delta

    cell = lax.broadcasted_iota(jnp.int32, (CS, block_count), 0)
    block = lax.broadcasted_iota(jnp.int32, (CS, block_count), 1)
    for copy in copies:
        copy.wait()
    blank = jnp.zeros((8, LANES), F32)
    products = []
    for k in range(4):
        line = deltas[2 + k // 2][:, LANES * (k & 1) : LANES * (k & 1) + LANES]
        x = jnp.concatenate([line, blank], axis=0).astype(BF16)
        tiles = jnp.concatenate([ends[k, 0], ends[k, 1]], axis=1)
        products.append(jnp.dot(x, tiles, preferred_element_type=F32))
    for k, b in enumerate((0, 1, block_count - 2, block_count - 1)):
        for t in (0, 1):
            rows = pl.ds(pl.multiple_of(window_ref[t, b] * 8, 8), 8)
            send_ref[owner_ref[t, b], rows, :] += products[k][0:8, LANES * t : LANES * t + LANES]
    values = sum(
        jnp.dot(
            deltas[s].astype(BF16),
            jnp.where(block == 2 * cell + s, 1.0, 0.0).astype(BF16),
            preferred_element_type=F32,
        )
        for s in (0, 1)
    )
    values = jnp.concatenate([values, values], axis=1)
    lines = line_ref[...].astype(BF16)
    targets = owners_ref[...] * WINDOWS + windows_ref[...]
    targets = jnp.concatenate([targets[0:1], targets[1:2]], axis=1)
    targets = jnp.broadcast_to(targets, values.shape)
    owners = send_ref.shape[0]
    wide = 4
    outs = []
    for o in range(0, owners, wide):
        rows = [
            jnp.where(targets == w, values, 0.0)
            for w in range(o * WINDOWS, (o + wide) * WINDOWS)
        ]
        columns = jnp.dot(
            jnp.concatenate(rows, axis=0).astype(BF16), lines, preferred_element_type=F32
        )
        for k in range(wide):
            send_ref[o + k, 0:32, :] += columns[32 * k : 32 * k + 32]
        spot = pl.ds(o, wide)
        sem = sems.at[8 + o // wide]
        outs.append(pltpu.make_async_copy(send_ref.at[spot], send_hbm.at[spot], sem))
        outs[-1].start()
    for out in outs:
        out.wait()


def fix_edges(source, turns, route, own, scale, part, line, edges, weights):
    return pl.pallas_call(
        fix_kernel,
        out_shape=(pltpu.HBM(part.shape, F32), jax.ShapeDtypeStruct((4, 8, CS), F32)),
        in_specs=[smem()] * 4 + [vmem()] * 4 + [anywhere()] + [hbm()] * 3,
        out_specs=(hbm(), vmem()),
        scratch_shapes=[
            pltpu.VMEM((4, 8, CS), F32),
            pltpu.VMEM((4, 2, LANES, LANES), BF16),
            pltpu.VMEM(line.shape, F32),
            pltpu.VMEM(part.shape, F32),
            pltpu.SemaphoreType.DMA((8 + part.shape[0] // 4,)),
        ],
        compiler_params=params(10),
        cost_estimate=cost(2 * 1024 * 1024 * 128, 3 << 20),
        name="edge_fix",
    )(
        source,
        turns,
        *route,
        *route,
        own,
        scale,
        edges,
        in_hbm(part),
        in_hbm(line),
        in_hbm(weights),
    )


def place_kernel(
    u_hbm,
    v_hbm,
    step_x_hbm,
    step_y_hbm,
    coriolis_hbm,
    lift_hbm,
    far_hbm,
    near_hbm,
    delta_ref,
    out_hbm,
    u_ref,
    v_ref,
    step_x_ref,
    step_y_ref,
    coriolis_ref,
    lift_ref,
    far_ref,
    near_ref,
    out_ref,
    cols,
    sems,
    out_sems,
):
    loads = half_loads(
        (u_hbm, v_hbm, step_x_hbm, step_y_hbm, coriolis_hbm, lift_hbm, far_hbm, near_hbm),
        (u_ref, v_ref, step_x_ref, step_y_ref, coriolis_ref, lift_ref, far_ref, near_ref),
        sems,
    )
    for load in loads[0] + loads[1]:
        load.start()
    cols[...] = jnp.transpose(
        jnp.concatenate(
            [delta_ref[0], delta_ref[1], jnp.zeros((LANES - 16, CS), F32)], axis=0
        )
    )
    lane = lax.broadcasted_iota(jnp.int32, (CHUNK, CS), 1)

    def put(r0, r, value):
        rows = pl.ds(r0, CHUNK)
        sides = cols[rows, :]
        left = jnp.where(lane == 0, sides[:, r : r + 1], 0.0)
        right = jnp.where(lane == CS - 1, sides[:, 8 + r : 9 + r], 0.0)
        out_ref[r // 4, r % 4, rows, :] = value + (left + right)

    inner = stencil_step(u_ref, v_ref, lift_ref, step_x_ref, step_y_ref, coriolis_ref, put)
    terms = outer_terms(lax.rem(lax.axis_index("lev"), 2), lift_ref, far_ref, near_ref)

    def step(c, carry):
        inner(c, carry)
        rows = pl.ds(pl.multiple_of(c * CHUNK, CHUNK), CHUNK)
        for comp, level, value in terms(rows):
            out_ref[comp, level, rows, :] += value
        return carry

    first, second = pl.ds(0, SPLIT * CHUNK), pl.ds(SPLIT * CHUNK, CS - SPLIT * CHUNK)
    outs = [
        pltpu.make_async_copy(out_ref.at[:, :, rows], out_hbm.at[:, :, rows], out_sems.at[k])
        for k, rows in enumerate((first, second))
    ]
    ends = ((0, SPLIT, 0, 2), (SPLIT, CS // CHUNK, CS - 1, 3))
    for h, (start, stop, line, side) in enumerate(ends):
        for load in loads[h]:
            load.wait()
        lax.fori_loop(start, stop, step, 0)
        for comp in (0, 1):
            for level in range(4):
                r = comp * 4 + level
                out_ref[comp, level, line : line + 1, :] += delta_ref[side, r : r + 1, :]
        outs[h].start()
    for out in outs:
        out.wait()


def place(fields, delta):
    return pl.pallas_call(
        place_kernel,
        out_shape=pltpu.HBM((2, 4, CS, CS), F32),
        in_specs=[hbm()] * len(fields) + [vmem()],
        out_specs=hbm(),
        scratch_shapes=[pltpu.VMEM(x.shape, F32) for x in fields]
        + [
            pltpu.VMEM((2, 4, CS, CS), F32),
            pltpu.VMEM((CS, LANES), F32),
            pltpu.SemaphoreType.DMA((2, len(fields))),
            pltpu.SemaphoreType.DMA((2,)),
        ],
        compiler_params=params(14),
        cost_estimate=cost(1 << 20, 8 << 20),
        name="place",
    )(*[in_hbm(x) for x in fields], delta)


def finish_kernel(got_ref, out_ref):
    total = got_ref[0]
    for d in range(1, got_ref.shape[0]):
        total = total + got_ref[d]
    for w in range(WINDOWS):
        share = total[8 * w : 8 * w + 8] / jnp.maximum(total[32 + w : 33 + w], 1.0)
        out_ref[0, :, LANES * w : LANES * w + LANES] = share[0:4]
        out_ref[1, :, LANES * w : LANES * w + LANES] = share[4:8]


def finish(got):
    return pl.pallas_call(
        finish_kernel,
        out_shape=jax.ShapeDtypeStruct((2, 4, WINDOWS * LANES), F32),
        in_specs=[vmem()],
        out_specs=vmem(),
        compiler_params=params(4),
        cost_estimate=cost(1000, 1 << 20),
        name="finish",
    )(got)


def per_device(
    wind_u,
    wind_v,
    vertical,
    spacing_x,
    spacing_y,
    coriolis,
    edge_source,
    edge_turns,
    route_owner,
    route_window,
    remap_weights,
):
    owners = lax.axis_size("sub")
    groups = lax.axis_size("lev")
    edges, own, far, near = take_edges(wind_u, wind_v, owners)
    odds = range(1, groups - 1, 2)
    far = lax.ppermute(far, "lev", [(i, i + 1) for i in odds] + [(i + 1, i) for i in odds])
    near = lax.ppermute(near, "lev", [(i, i ^ 1) for i in range(groups)])
    edges = lax.all_to_all(edges, "sub", split_axis=0, concat_axis=0, tiled=True)
    route = (route_owner.T, route_window.T)
    fields = (wind_u, wind_v, spacing_x, spacing_y, coriolis, vertical)
    blocks, scale, lift, held = inner_tendencies(fields, remap_weights)
    part, line, far, near = remap_inner(
        route, blocks, held, lift, far, near, remap_weights, owners
    )
    send, delta = fix_edges(
        edge_source, edge_turns, route, own, scale, part, line, edges, remap_weights
    )
    got = lax.all_to_all(send, "sub", split_axis=0, concat_axis=0, tiled=True)
    return place(fields + (far, near), delta), finish(in_vmem(got))


def solution(mesh):
    placed = (
        P("lev", "sub", None),
        P("lev", "sub", None),
        P("lev", "sub", None),
        P("sub", None),
        P("sub", None),
        P("sub", None),
        P("sub", None),
        P("sub", None),
        P("sub", None),
        P("sub", None),
        P("sub", None, None, None),
    )
    return jax.shard_map(
        per_device,
        mesh=mesh,
        in_specs=placed,
        out_specs=(P(None, "lev", "sub", None), P(None, "lev", "sub")),
        check_vma=False,
    )
```

```python
import jax
import jax.numpy as jnp
from jax import lax
from jax.experimental import pallas as pl
from jax.experimental.pallas import tpu as pltpu
from jax.sharding import PartitionSpec as P

WINDOWS = 4
CS = 256
LANES = 128
CHUNK = 16
ACCS = 4
GROUP = 32
PIECE = 32
WIDE = 4
HELD = 160
SPLIT = CS // CHUNK // 2 - 1
QUARTERS = 4
F32 = jnp.float32
BF16 = jnp.bfloat16


def vmem():
    return pl.BlockSpec(memory_space=pltpu.VMEM)


def smem():
    return pl.BlockSpec(memory_space=pltpu.SMEM)


def anywhere():
    return pl.BlockSpec(memory_space=pl.ANY)


def hbm():
    return pl.BlockSpec(memory_space=pltpu.HBM)


def in_hbm(x):
    return pltpu.with_memory_space_constraint(x, pltpu.HBM)


def in_vmem(x):
    return pltpu.with_memory_space_constraint(x, pltpu.VMEM)


def params(mib):
    return pltpu.CompilerParams(vmem_limit_bytes=mib * 1024 * 1024)


def cost(flops, size):
    return pl.CostEstimate(flops=flops, bytes_accessed=size, transcendentals=0)


def edge_kernel(
    wind_u,
    wind_v,
    step_x_hbm,
    step_y_hbm,
    coriolis_hbm,
    edges_ref,
    own_ref,
    far_ref,
    near_ref,
    u_ref,
    v_ref,
    step_x_ref,
    step_y_ref,
    coriolis_ref,
    held,
    in_sems,
    out_sems,
):
    loads, sends = [], []
    order = [(comp, level) for level in (0, 3, 1, 2) for comp in (0, 1)]
    winds, refs = (wind_u, wind_v), (u_ref, v_ref)
    for k, (comp, level) in enumerate(order):
        loads.append(
            pltpu.make_async_copy(winds[comp].at[level], refs[comp].at[level], in_sems.at[k])
        )
    for load in loads:
        load.start()
    sources, dests = (step_x_hbm, step_y_hbm, coriolis_hbm), (step_x_ref, step_y_ref, coriolis_ref)
    steps = [
        pltpu.make_async_copy(source, dest, in_sems.at[8 + k])
        for k, (source, dest) in enumerate(zip(sources, dests))
    ]
    for load in steps:
        load.start()
    lane = lax.broadcasted_iota(jnp.int32, (CS, LANES), 1)
    columns = jnp.zeros((CS, LANES), F32)
    for k, (comp, level) in enumerate(order):
        loads[k].wait()
        ref = refs[comp]
        if level in (0, 3):
            if level == 3:
                odd = lax.rem(lax.axis_index("lev"), 2)
                for n, (out, at) in enumerate(((far_ref, 3 * odd), (near_ref, 3 - 3 * odd))):
                    sem = out_sems.at[2 * comp + n]
                    sends.append(pltpu.make_async_copy(ref.at[at], out.at[comp], sem))
                    sends[-1].start()
        for side in (0, 1):
            at = 0 if side == 0 else CS - 1
            column = ref[level, :, pl.ds(at, 1)]
            columns = jnp.where(lane == side * 8 + comp * 4 + level, column, columns)
    owners = held.shape[0]
    lines = [ref[:, at, :] for at in (0, CS - 1) for ref in refs]
    for k, rows in ((1, lines), (0, None)):
        edges = jnp.concatenate(rows, axis=0) if rows else jnp.transpose(columns)[0:16, :]
        spot = pl.ds(16 * k, 16)
        for d in range(owners):
            held[d, spot, :] = edges
        for n in (0, 1):
            part = pl.ds(n * (owners // 2), owners // 2)
            source, dest = held.at[part, spot], edges_ref.at[part, spot]
            sends.append(pltpu.make_async_copy(source, dest, out_sems.at[5 + 2 * k + n]))
            sends[-1].start()
    sends.append(pltpu.make_async_copy(held.at[0], own_ref, out_sems.at[4]))
    sends[-1].start()
    for copy in sends + steps:
        copy.wait()


def take_edges(fields, owners):
    return pl.pallas_call(
        edge_kernel,
        out_shape=(
            pltpu.HBM((owners, 32, CS), F32),
            pltpu.HBM((32, CS), F32),
            pltpu.HBM((2, CS, CS), F32),
            pltpu.HBM((2, CS, CS), F32),
        )
        + tuple(pltpu.VMEM(x.shape, F32) for x in fields),
        in_specs=[hbm()] * 5,
        out_specs=(hbm(),) * 4 + (vmem(),) * 5,
        scratch_shapes=[
            pltpu.VMEM((owners, 32, CS), F32),
            pltpu.SemaphoreType.DMA((11,)),
            pltpu.SemaphoreType.DMA((9,)),
        ],
        compiler_params=params(5),
        cost_estimate=cost(1000, 4 << 20),
        name="edges",
    )(*[in_hbm(x) for x in fields])


def spread(blocks, r0, r, value):
    for part in range(value.shape[0] // 8):
        for h in (0, 1):
            start = (r0 + part * 8) * 16 + 8 * h + r
            blocks[pl.ds(start, 8, stride=16), :] = value[
                8 * part : 8 * part + 8, LANES * h : LANES * h + LANES
            ]


def half_loads(sources, dests, sems):
    halves = []
    for h in (0, 1):
        rows = pl.ds(h * (CS // 2), CS // 2)
        copies = []
        for k, (source, dest) in enumerate(zip(sources, dests)):
            if len(source.shape) == 3:
                source, dest = source.at[:, rows], dest.at[:, rows]
            else:
                source, dest = source.at[rows], dest.at[rows]
            copies.append(pltpu.make_async_copy(source, dest, sems.at[h, k]))
        halves.append(copies)
    return halves


def stencil_step(u_ref, v_ref, lift_ref, step_x_ref, step_y_ref, coriolis_ref, put):
    lane = lax.broadcasted_iota(jnp.int32, (CHUNK, CS), 1)
    inner_left, inner_right = lane > 0, lane < CS - 1
    chunks = CS // CHUNK

    def stencil(c, carry):
        r0 = pl.multiple_of(c * CHUNK, CHUNK)
        before = pl.multiple_of(jnp.maximum(r0 - 8, 0), 8)
        after = pl.multiple_of(jnp.minimum(r0 + CHUNK, CS - 8), 8)
        rows = pl.ds(r0, CHUNK)
        half_x = 0.5 / step_x_ref[rows, :]
        half_y = 0.5 / step_y_ref[rows, :]
        rotation = coriolis_ref[rows, :]

        def ends(ref, level):
            top = jnp.where(c == 0, 0.0, ref[level, pl.ds(before, 8), :][7:8])
            bottom = jnp.where(c == chunks - 1, 0.0, ref[level, pl.ds(after, 8), :][0:1])
            return top, bottom

        def rise(mid, top, bottom):
            return jnp.concatenate([mid[1:], bottom], axis=0) - jnp.concatenate(
                [top, mid[: CHUNK - 1]], axis=0
            )

        def across(mid):
            return jnp.where(inner_right, pltpu.roll(mid, CS - 1, 1), 0.0) - jnp.where(
                inner_left, pltpu.roll(mid, 1, 1), 0.0
            )

        def energy(a, b):
            return 0.5 * (a * a + b * b)

        for level in range(4):
            u, v = u_ref[level, rows, :], v_ref[level, rows, :]
            top_u, bottom_u = ends(u_ref, level)
            top_v, bottom_v = ends(v_ref, level)
            kinetic = energy(u, v)
            vort = across(v) * half_x - rise(u, top_u, bottom_u) * half_y + rotation
            slope_x = across(kinetic) * half_x
            slope_y = rise(kinetic, energy(top_u, top_v), energy(bottom_u, bottom_v)) * half_y
            lift = lift_ref[level, rows, :] * 0.5
            if level == 0:
                shear_u, shear_v = u_ref[1, rows, :], v_ref[1, rows, :]
            elif level == 3:
                shear_u, shear_v = -u_ref[2, rows, :], -v_ref[2, rows, :]
            else:
                shear_u = u_ref[level + 1, rows, :] - u_ref[level - 1, rows, :]
                shear_v = v_ref[level + 1, rows, :] - v_ref[level - 1, rows, :]
            put(r0, level, vort * v - slope_x - lift * shear_u)
            put(r0, 4 + level, -vort * u - slope_y - lift * shear_v)
        return carry

    return stencil


def stencil_kernel(
    u_ref,
    v_ref,
    step_x_ref,
    step_y_ref,
    coriolis_ref,
    lift_hbm,
    weights_hbm,
    blocks,
    scale_ref,
    lift_ref,
    held_ref,
    field_sems,
    sems,
):
    loads = half_loads((lift_hbm,), (lift_ref,), field_sems)
    for load in loads[0] + loads[1]:
        load.start()
    copies = []
    for k in range(HELD // PIECE):
        part = pl.ds(k * PIECE, PIECE)
        copies.append(pltpu.make_async_copy(weights_hbm.at[part], held_ref.at[part], sems.at[k]))
    step = stencil_step(
        u_ref, v_ref, lift_ref, step_x_ref, step_y_ref, coriolis_ref, lambda *at: spread(blocks, *at)
    )
    for load in loads[0]:
        load.wait()
    for copy in copies:
        copy.start()
    lax.fori_loop(0, CS // CHUNK // 2, step, 0)
    for load in loads[1]:
        load.wait()
    lax.fori_loop(CS // CHUNK // 2, CS // CHUNK, step, 0)
    side = lax.broadcasted_iota(jnp.int32, (CS, LANES), 1)
    columns = jnp.where(side == 0, step_x_ref[:, 0:1], step_x_ref[:, CS - 1 : CS])
    steps = jnp.concatenate(
        [
            jnp.transpose(columns)[0:2],
            step_y_ref[0:1, :],
            step_y_ref[CS - 1 : CS, :],
            jnp.ones((4, CS), F32),
        ],
        axis=0,
    )
    scale_ref[...] = 0.5 / steps
    for copy in copies:
        copy.wait()


def inner_tendencies(fields, lift, weights):
    return pl.pallas_call(
        stencil_kernel,
        out_shape=(
            pltpu.VMEM((CS * 16, LANES), F32),
            pltpu.HBM((8, CS), F32),
            pltpu.VMEM((4, CS, CS), F32),
            pltpu.VMEM((HELD,) + weights.shape[1:], BF16),
        ),
        in_specs=[vmem()] * 5 + [hbm()] * 2,
        out_specs=(vmem(),) * 4,
        scratch_shapes=[
            pltpu.SemaphoreType.DMA((2, 1)),
            pltpu.SemaphoreType.DMA((HELD // PIECE,)),
        ],
        compiler_params=params(10),
        cost_estimate=cost(0, 0),
        name="stencil",
    )(*[in_vmem(x) for x in fields], in_hbm(lift), in_hbm(weights))


def outer_terms(odd, lift_ref, far_ref, near_ref):
    sides = ((far_ref, 3 * odd, odd), (near_ref, 3 - 3 * odd, 1 - odd))

    def terms(rows):
        out = []
        for ref, level, top in sides:
            lift = lift_ref[level, rows, :] * jnp.where(top == 1, -0.5, 0.5)
            out += [(comp, level, lift * ref[comp, rows, :]) for comp in (0, 1)]
        return out

    return terms


def remap_kernel(
    owner_ref,
    window_ref,
    blocks_in,
    held_ref,
    lift_ref,
    far_ref,
    near_ref,
    weights_hbm,
    part_hbm,
    line_hbm,
    far_hbm,
    near_hbm,
    part_ref,
    blocks,
    line_ref,
    rest_ref,
    *rest,
):
    accs, (sems, in_sems) = rest[:ACCS], rest[ACCS:]
    block_count = weights_hbm.shape[0]
    steps = block_count // GROUP
    held_steps = HELD // GROUP
    lines = GROUP // 2

    def load(c):
        source = weights_hbm.at[pl.ds(HELD + c * PIECE, PIECE)]
        return pltpu.make_async_copy(source, rest_ref.at[pl.ds(c * PIECE, PIECE)], sems.at[c])

    for acc in accs:
        acc[...] = jnp.zeros_like(acc)
    for c in range((block_count - HELD) // PIECE):
        load(c).start()
    outs = [
        pltpu.make_async_copy(far_ref, far_hbm, in_sems.at[3]),
        pltpu.make_async_copy(near_ref, near_hbm, in_sems.at[4]),
    ]
    for out in outs:
        out.start()
    odd = lax.rem(lax.axis_index("lev"), 2)
    terms = outer_terms(odd, lift_ref, far_ref, near_ref)

    def levels(r0):
        part = pl.ds(pl.multiple_of(r0 * 16, 128), 128)
        blocks[part, :] = blocks_in[part, :]
        for comp, level, value in terms(pl.ds(r0, 8)):
            for h in (0, 1):
                spot = pl.ds(r0 * 16 + 8 * h + comp * 4 + level, 8, stride=16)
                half = value[:, LANES * h : LANES * h + LANES]
                blocks[spot, :] = blocks_in[spot, :] + half

    row = lax.broadcasted_iota(jnp.int32, (8, LANES), 0)
    lane = lax.broadcasted_iota(jnp.int32, (8, LANES), 1)
    ones = jnp.where(row == 0, 1.0, 0.0)
    extra = [jnp.where((row == 1) & (lane == q), 1.0, ones) for q in (0, LANES - 1)]

    def remap(c, weights_ref, first_block):
        for k in range(lines // 8):
            levels(pl.multiple_of(c * lines + 8 * k, 8))
        parts, targets = [], []
        for k in range(GROUP):
            b = c * GROUP + k
            x = blocks[pl.ds(pl.multiple_of(b * 8, 8), 8), :]
            x = jnp.concatenate([x, extra[k & 1]], axis=0).astype(BF16)
            here = b - first_block
            tiles = jnp.concatenate([weights_ref[here, 0], weights_ref[here, 1]], axis=1)
            product = jnp.dot(x, tiles, preferred_element_type=F32)
            for t in (0, 1):
                half = product[:, LANES * t : LANES * t + LANES]
                parts.append(half)
                targets.append(owner_ref[t, b] * WINDOWS + window_ref[t, b])
                line_ref[pl.ds(t * block_count + b, 1), :] = half[9:10]
        for first in range(0, len(parts), ACCS):
            here = range(first, first + ACCS)
            olds = [accs[i - first][targets[i]] for i in here]
            for i, old in zip(here, olds):
                accs[i - first][targets[i]] = old + parts[i]

    def remap_held(c, carry):
        remap(c, held_ref, 0)
        return carry

    def remap_rest(c, carry):
        for k in range(GROUP // PIECE):
            load((c - held_steps) * (GROUP // PIECE) + k).wait()
        remap(c, rest_ref, HELD)
        return carry

    lax.fori_loop(0, held_steps, remap_held, 0)
    lax.fori_loop(held_steps, steps, remap_rest, 0)
    line_out = pltpu.make_async_copy(line_ref, line_hbm, in_sems.at[2])
    line_out.start()

    def gather(o, carry):
        sums = []
        for w in range(WINDOWS):
            total = accs[0][o * WINDOWS + w]
            for acc in accs[1:]:
                total = total + acc[o * WINDOWS + w]
            part_ref[o, w * 8 : w * 8 + 8, :] = total[0:8]
            sums.append(total[8:9])
        part_ref[o, 32:40, :] = jnp.concatenate(sums + [jnp.zeros((4, LANES), F32)], axis=0)
        return carry

    size = part_ref.shape[0] // QUARTERS
    for k in range(QUARTERS):
        lax.fori_loop(k * size, (k + 1) * size, gather, 0)
        spot = pl.ds(k * size, size)
        outs.append(pltpu.make_async_copy(part_ref.at[spot], part_hbm.at[spot], in_sems.at[5 + k]))
        outs[-1].start()
    for out in outs + [line_out]:
        out.wait()


def remap_inner(route, blocks, held, lift, far, near, weights, owners):
    count = weights.shape[0]
    return pl.pallas_call(
        remap_kernel,
        out_shape=(
            pltpu.HBM((owners, 40, LANES), F32),
            pltpu.HBM((2 * count, LANES), F32),
            pltpu.HBM((2, CS, CS), F32),
            pltpu.HBM((2, CS, CS), F32),
        ),
        in_specs=[smem()] * 2 + [vmem()] * 5 + [hbm()],
        out_specs=(hbm(),) * 4,
        scratch_shapes=[
            pltpu.VMEM((owners, 40, LANES), F32),
            pltpu.VMEM(blocks.shape, F32),
            pltpu.VMEM((2 * count, LANES), F32),
            pltpu.VMEM((count - HELD,) + weights.shape[1:], BF16),
        ]
        + [pltpu.VMEM((owners * WINDOWS, 16, LANES), F32)] * ACCS
        + [
            pltpu.SemaphoreType.DMA(((count - HELD) // PIECE,)),
            pltpu.SemaphoreType.DMA((5 + QUARTERS,)),
        ],
        compiler_params=params(36),
        cost_estimate=cost(10**15, 1 << 40),
        name="remap",
    )(
        *route,
        *[in_vmem(x) for x in (blocks, held, lift)],
        far,
        near,
        in_hbm(weights),
    )


def reverse_lanes(x):
    rows = x.shape[0]
    i = lax.broadcasted_iota(jnp.int32, (CS, CS), 0)
    j = lax.broadcasted_iota(jnp.int32, (CS, CS), 1)
    flip = jnp.where(i + j == CS - 1, 1.0, 0.0).astype(BF16)
    high = x.astype(BF16)
    rest = x - high.astype(F32)
    mid = rest.astype(BF16)
    low = (rest - mid.astype(F32)).astype(BF16)
    parts = jnp.dot(jnp.concatenate([high, mid, low], axis=0), flip, preferred_element_type=F32)
    return parts[0:rows] + parts[rows : 2 * rows] + parts[2 * rows : 3 * rows]


def fix_kernel(
    source_ref,
    turns_ref,
    owner_ref,
    window_ref,
    owners_ref,
    windows_ref,
    own_ref,
    scale_ref,
    edges_any,
    part_hbm,
    line_hbm,
    weights_hbm,
    send_hbm,
    delta_ref,
    got,
    ends,
    line_ref,
    send_ref,
    sems,
):
    edge_copies, copies = [], []
    for s in range(4):
        e = source_ref[0, s]
        spot = edges_any.at[e >> 2, pl.ds(pl.multiple_of((e & 3) * 8, 8), 8)]
        edge_copies.append(pltpu.make_async_copy(spot, got.at[s], sems.at[s]))
    block_count = weights_hbm.shape[0]
    for k, at in enumerate((0, block_count - 2)):
        copies.append(
            pltpu.make_async_copy(
                weights_hbm.at[pl.ds(at, 2)], ends.at[pl.ds(2 * k, 2)], sems.at[4 + k]
            )
        )
    copies.append(pltpu.make_async_copy(line_hbm, line_ref, sems.at[6]))
    copies.append(pltpu.make_async_copy(part_hbm, send_ref, sems.at[7]))
    for copy in edge_copies + copies:
        copy.start()
    for copy in edge_copies:
        copy.wait()

    upper = lax.broadcasted_iota(jnp.int32, (8, CS), 0) < 4
    sign = jnp.where(upper, -1.0, 1.0)
    turned = []
    for s in range(4):
        k = turns_ref[0, s]
        cosine = jnp.where(k == 0, 1.0, 0.0) - jnp.where(k == 2, 1.0, 0.0)
        sine = jnp.where(k == 1, 1.0, 0.0) - jnp.where(k == 3, 1.0, 0.0)
        edge = got[s]
        turned.append(cosine * edge + sine * (sign * pltpu.roll(edge, 4, 0)))
    flipped = reverse_lanes(jnp.concatenate(turned, axis=0))
    deltas = []
    for s in range(4):
        odd = (turns_ref[0, s] & 1) == 1
        halo = jnp.where(odd, flipped[8 * s : 8 * s + 8], turned[s])
        other = pltpu.roll(halo, 4, 0)
        energy = 0.5 * (halo * halo + other * other)
        out = -1.0 if s in (0, 3) else 1.0
        half = scale_ref[s : s + 1, :]
        if s < 2:
            vort = out * half * jnp.where(upper, other, halo)
            kinetic = jnp.where(upper, -out * half * energy, 0.0)
        else:
            vort = out * half * jnp.where(upper, halo, other)
            kinetic = jnp.where(upper, 0.0, out * half * energy)
        across = pltpu.roll(own_ref[8 * s : 8 * s + 8, :], 4, 0)
        delta = kinetic - sign * vort * across
        deltas.append(delta)
        delta_ref[s] = delta

    cell = lax.broadcasted_iota(jnp.int32, (CS, block_count), 0)
    block = lax.broadcasted_iota(jnp.int32, (CS, block_count), 1)
    for copy in copies:
        copy.wait()
    blank = jnp.zeros((8, LANES), F32)
    products = []
    for k in range(4):
        line = deltas[2 + k // 2][:, LANES * (k & 1) : LANES * (k & 1) + LANES]
        x = jnp.concatenate([line, blank], axis=0).astype(BF16)
        tiles = jnp.concatenate([ends[k, 0], ends[k, 1]], axis=1)
        products.append(jnp.dot(x, tiles, preferred_element_type=F32))
    for k, b in enumerate((0, 1, block_count - 2, block_count - 1)):
        for t in (0, 1):
            rows = pl.ds(pl.multiple_of(window_ref[t, b] * 8, 8), 8)
            send_ref[owner_ref[t, b], rows, :] += products[k][0:8, LANES * t : LANES * t + LANES]
    values = sum(
        jnp.dot(
            deltas[s].astype(BF16),
            jnp.where(block == 2 * cell + s, 1.0, 0.0).astype(BF16),
            preferred_element_type=F32,
        )
        for s in (0, 1)
    )
    values = jnp.concatenate([values, values], axis=1)
    lines = line_ref[...].astype(BF16)
    targets = owners_ref[...] * WINDOWS + windows_ref[...]
    targets = jnp.concatenate([targets[0:1], targets[1:2]], axis=1)
    targets = jnp.broadcast_to(targets, values.shape)
    owners = send_ref.shape[0]
    wide = WIDE
    outs = []
    for o in range(0, owners, wide):
        rows = [
            jnp.where(targets == w, values, 0.0)
            for w in range(o * WINDOWS, (o + wide) * WINDOWS)
        ]
        columns = jnp.dot(
            jnp.concatenate(rows, axis=0).astype(BF16), lines, preferred_element_type=F32
        )
        for k in range(wide):
            send_ref[o + k, 0:32, :] += columns[32 * k : 32 * k + 32]
        spot = pl.ds(o, wide)
        sem = sems.at[8 + o // wide]
        outs.append(pltpu.make_async_copy(send_ref.at[spot], send_hbm.at[spot], sem))
        outs[-1].start()
    for out in outs:
        out.wait()


def fix_edges(source, turns, route, own, scale, part, line, edges, weights):
    return pl.pallas_call(
        fix_kernel,
        out_shape=(pltpu.HBM(part.shape, F32), jax.ShapeDtypeStruct((4, 8, CS), F32)),
        in_specs=[smem()] * 4 + [vmem()] * 4 + [anywhere()] + [hbm()] * 3,
        out_specs=(hbm(), vmem()),
        scratch_shapes=[
            pltpu.VMEM((4, 8, CS), F32),
            pltpu.VMEM((4, 2, LANES, LANES), BF16),
            pltpu.VMEM(line.shape, F32),
            pltpu.VMEM(part.shape, F32),
            pltpu.SemaphoreType.DMA((8 + part.shape[0] // WIDE,)),
        ],
        compiler_params=params(10),
        cost_estimate=cost(2 * 1024 * 1024 * 128, 3 << 20),
        name="edge_fix",
    )(
        source,
        turns,
        *route,
        *route,
        own,
        scale,
        edges,
        in_hbm(part),
        in_hbm(line),
        in_hbm(weights),
    )


def place_kernel(
    u_hbm,
    v_hbm,
    step_x_hbm,
    step_y_hbm,
    coriolis_hbm,
    lift_hbm,
    far_hbm,
    near_hbm,
    delta_ref,
    out_hbm,
    u_ref,
    v_ref,
    step_x_ref,
    step_y_ref,
    coriolis_ref,
    lift_ref,
    far_ref,
    near_ref,
    out_ref,
    cols,
    sems,
    out_sems,
):
    loads = half_loads(
        (u_hbm, v_hbm, step_x_hbm, step_y_hbm, coriolis_hbm, lift_hbm, far_hbm, near_hbm),
        (u_ref, v_ref, step_x_ref, step_y_ref, coriolis_ref, lift_ref, far_ref, near_ref),
        sems,
    )
    for load in loads[0] + loads[1]:
        load.start()
    cols[...] = jnp.transpose(
        jnp.concatenate(
            [delta_ref[0], delta_ref[1], jnp.zeros((LANES - 16, CS), F32)], axis=0
        )
    )
    lane = lax.broadcasted_iota(jnp.int32, (CHUNK, CS), 1)

    def put(r0, r, value):
        rows = pl.ds(r0, CHUNK)
        sides = cols[rows, :]
        left = jnp.where(lane == 0, sides[:, r : r + 1], 0.0)
        right = jnp.where(lane == CS - 1, sides[:, 8 + r : 9 + r], 0.0)
        out_ref[r // 4, r % 4, rows, :] = value + (left + right)

    inner = stencil_step(u_ref, v_ref, lift_ref, step_x_ref, step_y_ref, coriolis_ref, put)
    terms = outer_terms(lax.rem(lax.axis_index("lev"), 2), lift_ref, far_ref, near_ref)

    def step(c, carry):
        inner(c, carry)
        rows = pl.ds(pl.multiple_of(c * CHUNK, CHUNK), CHUNK)
        for comp, level, value in terms(rows):
            out_ref[comp, level, rows, :] += value
        return carry

    first, second = pl.ds(0, SPLIT * CHUNK), pl.ds(SPLIT * CHUNK, CS - SPLIT * CHUNK)
    outs = [
        pltpu.make_async_copy(out_ref.at[:, :, rows], out_hbm.at[:, :, rows], out_sems.at[k])
        for k, rows in enumerate((first, second))
    ]
    ends = ((0, SPLIT, 0, 2), (SPLIT, CS // CHUNK, CS - 1, 3))
    for h, (start, stop, line, side) in enumerate(ends):
        for load in loads[h]:
            load.wait()
        lax.fori_loop(start, stop, step, 0)
        for comp in (0, 1):
            for level in range(4):
                r = comp * 4 + level
                out_ref[comp, level, line : line + 1, :] += delta_ref[side, r : r + 1, :]
        outs[h].start()
    for out in outs:
        out.wait()


def place(fields, delta):
    return pl.pallas_call(
        place_kernel,
        out_shape=pltpu.HBM((2, 4, CS, CS), F32),
        in_specs=[hbm()] * len(fields) + [vmem()],
        out_specs=hbm(),
        scratch_shapes=[pltpu.VMEM(x.shape, F32) for x in fields]
        + [
            pltpu.VMEM((2, 4, CS, CS), F32),
            pltpu.VMEM((CS, LANES), F32),
            pltpu.SemaphoreType.DMA((2, len(fields))),
            pltpu.SemaphoreType.DMA((2,)),
        ],
        compiler_params=params(14),
        cost_estimate=cost(1 << 20, 8 << 20),
        name="place",
    )(*[in_hbm(x) for x in fields], delta)


def finish_kernel(got_ref, out_ref):
    total = got_ref[0]
    for d in range(1, got_ref.shape[0]):
        total = total + got_ref[d]
    for w in range(WINDOWS):
        share = total[8 * w : 8 * w + 8] / jnp.maximum(total[32 + w : 33 + w], 1.0)
        out_ref[0, :, LANES * w : LANES * w + LANES] = share[0:4]
        out_ref[1, :, LANES * w : LANES * w + LANES] = share[4:8]


def finish(got):
    return pl.pallas_call(
        finish_kernel,
        out_shape=jax.ShapeDtypeStruct((2, 4, WINDOWS * LANES), F32),
        in_specs=[vmem()],
        out_specs=vmem(),
        compiler_params=params(4),
        cost_estimate=cost(1000, 1 << 20),
        name="finish",
    )(got)


def per_device(
    wind_u,
    wind_v,
    vertical,
    spacing_x,
    spacing_y,
    coriolis,
    edge_source,
    edge_turns,
    route_owner,
    route_window,
    remap_weights,
):
    owners = lax.axis_size("sub")
    groups = lax.axis_size("lev")
    fields = (wind_u, wind_v, spacing_x, spacing_y, coriolis)
    edges, own, far, near, *held_fields = take_edges(fields, owners)
    odds = range(1, groups - 1, 2)
    far = lax.ppermute(far, "lev", [(i, i + 1) for i in odds] + [(i + 1, i) for i in odds])
    near = lax.ppermute(near, "lev", [(i, i ^ 1) for i in range(groups)])
    edges = lax.all_to_all(edges, "sub", split_axis=0, concat_axis=0, tiled=True)
    route = (route_owner.T, route_window.T)
    blocks, scale, lift, held = inner_tendencies(held_fields, vertical, remap_weights)
    part, line, far, near = remap_inner(
        route, blocks, held, lift, far, near, remap_weights, owners
    )
    send, delta = fix_edges(
        edge_source, edge_turns, route, own, scale, part, line, edges, remap_weights
    )
    got = lax.all_to_all(send, "sub", split_axis=0, concat_axis=0, tiled=True)
    return place(fields + (vertical, far, near), delta), finish(in_vmem(got))


def solution(mesh):
    placed = (
        P("lev", "sub", None),
        P("lev", "sub", None),
        P("lev", "sub", None),
        P("sub", None),
        P("sub", None),
        P("sub", None),
        P("sub", None),
        P("sub", None),
        P("sub", None),
        P("sub", None),
        P("sub", None, None, None),
    )
    return jax.shard_map(
        per_device,
        mesh=mesh,
        in_specs=placed,
        out_specs=(P(None, "lev", "sub", None), P(None, "lev", "sub")),
        check_vma=False,
    )
```

```python
import jax
import jax.numpy as jnp
from jax import lax
from jax.experimental import pallas as pl
from jax.experimental.pallas import tpu as pltpu
from jax.sharding import PartitionSpec as P

WINDOWS = 4
CS = 256
LANES = 128
CHUNK = 16
ACCS = 4
GROUP = 64
PIECE = 32
WIDE = 4
SPLIT = CS // CHUNK // 2 - 1
QUARTERS = 4
F32 = jnp.float32
BF16 = jnp.bfloat16


def vmem():
    return pl.BlockSpec(memory_space=pltpu.VMEM)


def smem():
    return pl.BlockSpec(memory_space=pltpu.SMEM)


def anywhere():
    return pl.BlockSpec(memory_space=pl.ANY)


def hbm():
    return pl.BlockSpec(memory_space=pltpu.HBM)


def in_hbm(x):
    return pltpu.with_memory_space_constraint(x, pltpu.HBM)


def in_vmem(x):
    return pltpu.with_memory_space_constraint(x, pltpu.VMEM)


def params(mib):
    return pltpu.CompilerParams(vmem_limit_bytes=mib * 1024 * 1024)


def cost(flops, size):
    return pl.CostEstimate(flops=flops, bytes_accessed=size, transcendentals=0)


def edge_kernel(
    wind_u,
    wind_v,
    edges_ref,
    own_ref,
    far_ref,
    near_ref,
    u_ref,
    v_ref,
    held,
    in_sems,
    out_sems,
):
    loads, sends = [], []
    order = [(comp, level) for level in (0, 3, 1, 2) for comp in (0, 1)]
    winds, refs = (wind_u, wind_v), (u_ref, v_ref)
    for k, (comp, level) in enumerate(order):
        loads.append(
            pltpu.make_async_copy(winds[comp].at[level], refs[comp].at[level], in_sems.at[k])
        )
    for load in loads:
        load.start()
    lane = lax.broadcasted_iota(jnp.int32, (CS, LANES), 1)
    columns = jnp.zeros((CS, LANES), F32)
    for k, (comp, level) in enumerate(order):
        loads[k].wait()
        ref = refs[comp]
        if level in (0, 3):
            if level == 3:
                odd = lax.rem(lax.axis_index("lev"), 2)
                for n, (out, at) in enumerate(((far_ref, 3 * odd), (near_ref, 3 - 3 * odd))):
                    sem = out_sems.at[2 * comp + n]
                    sends.append(pltpu.make_async_copy(ref.at[at], out.at[comp], sem))
                    sends[-1].start()
        for side in (0, 1):
            at = 0 if side == 0 else CS - 1
            column = ref[level, :, pl.ds(at, 1)]
            columns = jnp.where(lane == side * 8 + comp * 4 + level, column, columns)
    owners = held.shape[0]
    lines = [ref[:, at, :] for at in (0, CS - 1) for ref in refs]
    for k, rows in ((1, lines), (0, None)):
        edges = jnp.concatenate(rows, axis=0) if rows else jnp.transpose(columns)[0:16, :]
        spot = pl.ds(16 * k, 16)
        for d in range(owners):
            held[d, spot, :] = edges
        for n in (0, 1):
            part = pl.ds(n * (owners // 2), owners // 2)
            source, dest = held.at[part, spot], edges_ref.at[part, spot]
            sends.append(pltpu.make_async_copy(source, dest, out_sems.at[5 + 2 * k + n]))
            sends[-1].start()
    sends.append(pltpu.make_async_copy(held.at[0], own_ref, out_sems.at[4]))
    sends[-1].start()
    for copy in sends:
        copy.wait()


def take_edges(fields, owners):
    return pl.pallas_call(
        edge_kernel,
        out_shape=(
            pltpu.HBM((owners, 32, CS), F32),
            pltpu.HBM((32, CS), F32),
            pltpu.HBM((2, CS, CS), F32),
            pltpu.HBM((2, CS, CS), F32),
        )
        + tuple(pltpu.VMEM(x.shape, F32) for x in fields),
        in_specs=[hbm()] * 2,
        out_specs=(hbm(),) * 4 + (vmem(),) * 2,
        scratch_shapes=[
            pltpu.VMEM((owners, 32, CS), F32),
            pltpu.SemaphoreType.DMA((11,)),
            pltpu.SemaphoreType.DMA((9,)),
        ],
        compiler_params=params(5),
        cost_estimate=cost(1000, 4 << 20),
        name="edges",
    )(*[in_hbm(x) for x in fields])


def spread(blocks, r0, r, value):
    for part in range(value.shape[0] // 8):
        for h in (0, 1):
            start = (r0 + part * 8) * 16 + 8 * h + r
            blocks[pl.ds(start, 8, stride=16), :] = value[
                8 * part : 8 * part + 8, LANES * h : LANES * h + LANES
            ]


def half_loads(sources, dests, sems):
    halves = []
    for h in (0, 1):
        rows = pl.ds(h * (CS // 2), CS // 2)
        copies = []
        for k, (source, dest) in enumerate(zip(sources, dests)):
            if len(source.shape) == 3:
                source, dest = source.at[:, rows], dest.at[:, rows]
            else:
                source, dest = source.at[rows], dest.at[rows]
            copies.append(pltpu.make_async_copy(source, dest, sems.at[h, k]))
        halves.append(copies)
    return halves


def stencil_step(u_ref, v_ref, lift_ref, step_x_ref, step_y_ref, coriolis_ref, put):
    lane = lax.broadcasted_iota(jnp.int32, (CHUNK, CS), 1)
    inner_left, inner_right = lane > 0, lane < CS - 1
    chunks = CS // CHUNK

    def stencil(c, carry):
        r0 = pl.multiple_of(c * CHUNK, CHUNK)
        before = pl.multiple_of(jnp.maximum(r0 - 8, 0), 8)
        after = pl.multiple_of(jnp.minimum(r0 + CHUNK, CS - 8), 8)
        rows = pl.ds(r0, CHUNK)
        half_x = 0.5 / step_x_ref[rows, :]
        half_y = 0.5 / step_y_ref[rows, :]
        rotation = coriolis_ref[rows, :]

        def ends(ref, level):
            top = jnp.where(c == 0, 0.0, ref[level, pl.ds(before, 8), :][7:8])
            bottom = jnp.where(c == chunks - 1, 0.0, ref[level, pl.ds(after, 8), :][0:1])
            return top, bottom

        def rise(mid, top, bottom):
            return jnp.concatenate([mid[1:], bottom], axis=0) - jnp.concatenate(
                [top, mid[: CHUNK - 1]], axis=0
            )

        def across(mid):
            return jnp.where(inner_right, pltpu.roll(mid, CS - 1, 1), 0.0) - jnp.where(
                inner_left, pltpu.roll(mid, 1, 1), 0.0
            )

        def energy(a, b):
            return 0.5 * (a * a + b * b)

        for level in range(4):
            u, v = u_ref[level, rows, :], v_ref[level, rows, :]
            top_u, bottom_u = ends(u_ref, level)
            top_v, bottom_v = ends(v_ref, level)
            kinetic = energy(u, v)
            vort = across(v) * half_x - rise(u, top_u, bottom_u) * half_y + rotation
            slope_x = across(kinetic) * half_x
            slope_y = rise(kinetic, energy(top_u, top_v), energy(bottom_u, bottom_v)) * half_y
            lift = lift_ref[level, rows, :] * 0.5
            if level == 0:
                shear_u, shear_v = u_ref[1, rows, :], v_ref[1, rows, :]
            elif level == 3:
                shear_u, shear_v = -u_ref[2, rows, :], -v_ref[2, rows, :]
            else:
                shear_u = u_ref[level + 1, rows, :] - u_ref[level - 1, rows, :]
                shear_v = v_ref[level + 1, rows, :] - v_ref[level - 1, rows, :]
            put(r0, level, vort * v - slope_x - lift * shear_u)
            put(r0, 4 + level, -vort * u - slope_y - lift * shear_v)
        return carry

    return stencil


def outer_terms(odd, lift_ref, far_ref, near_ref):
    sides = ((far_ref, 3 * odd, odd), (near_ref, 3 - 3 * odd, 1 - odd))

    def terms(rows):
        out = []
        for ref, level, top in sides:
            lift = lift_ref[level, rows, :] * jnp.where(top == 1, -0.5, 0.5)
            out += [(comp, level, lift * ref[comp, rows, :]) for comp in (0, 1)]
        return out

    return terms


def remap_kernel(
    owner_hbm,
    window_hbm,
    u_ref,
    v_ref,
    step_x_hbm,
    step_y_hbm,
    coriolis_hbm,
    lift_hbm,
    far_any,
    near_any,
    weights_hbm,
    scale_ref,
    part_hbm,
    line_hbm,
    far_hbm,
    near_hbm,
    part_ref,
    blocks,
    line_ref,
    owner_ref,
    window_ref,
    step_x_ref,
    step_y_ref,
    coriolis_ref,
    lift_ref,
    far_ref,
    near_ref,
    weights_ref,
    *rest,
):
    accs, (sems, in_sems, field_sems) = rest[:ACCS], rest[ACCS:]
    block_count = weights_hbm.shape[0]
    steps = block_count // GROUP
    lines = GROUP // 2
    loads = half_loads(
        (step_x_hbm, step_y_hbm, coriolis_hbm, lift_hbm),
        (step_x_ref, step_y_ref, coriolis_ref, lift_ref),
        field_sems,
    )
    firsts = [
        pltpu.make_async_copy(owner_hbm, owner_ref, in_sems.at[2]),
        pltpu.make_async_copy(window_hbm, window_ref, in_sems.at[5 + QUARTERS]),
        pltpu.make_async_copy(far_any, far_ref, in_sems.at[0]),
        pltpu.make_async_copy(near_any, near_ref, in_sems.at[1]),
    ]
    for copy in loads[0] + loads[1] + firsts:
        copy.start()

    def load(c):
        part = pl.ds(c * PIECE, PIECE)
        return pltpu.make_async_copy(weights_hbm.at[part], weights_ref.at[part], sems.at[c])

    for acc in accs:
        acc[...] = jnp.zeros_like(acc)
    step = stencil_step(
        u_ref, v_ref, lift_ref, step_x_ref, step_y_ref, coriolis_ref, lambda *at: spread(blocks, *at)
    )
    for copy in loads[0]:
        copy.wait()
    for c in range(block_count // PIECE):
        load(c).start()
    lax.fori_loop(0, CS // CHUNK // 2, step, 0)
    for copy in loads[1]:
        copy.wait()
    lax.fori_loop(CS // CHUNK // 2, CS // CHUNK, step, 0)
    side = lax.broadcasted_iota(jnp.int32, (CS, LANES), 1)
    columns = jnp.where(side == 0, step_x_ref[:, 0:1], step_x_ref[:, CS - 1 : CS])
    ends = jnp.concatenate(
        [
            jnp.transpose(columns)[0:2],
            step_y_ref[0:1, :],
            step_y_ref[CS - 1 : CS, :],
            jnp.ones((4, CS), F32),
        ],
        axis=0,
    )
    scale_ref[...] = 0.5 / ends
    for copy in firsts:
        copy.wait()
    outs = [
        pltpu.make_async_copy(far_ref, far_hbm, in_sems.at[3]),
        pltpu.make_async_copy(near_ref, near_hbm, in_sems.at[4]),
    ]
    for out in outs:
        out.start()
    odd = lax.rem(lax.axis_index("lev"), 2)
    terms = outer_terms(odd, lift_ref, far_ref, near_ref)

    def levels(r0):
        for comp, level, value in terms(pl.ds(r0, 8)):
            for h in (0, 1):
                spot = pl.ds(r0 * 16 + 8 * h + comp * 4 + level, 8, stride=16)
                half = value[:, LANES * h : LANES * h + LANES]
                blocks[spot, :] = blocks[spot, :] + half

    row = lax.broadcasted_iota(jnp.int32, (8, LANES), 0)
    lane = lax.broadcasted_iota(jnp.int32, (8, LANES), 1)
    ones = jnp.where(row == 0, 1.0, 0.0)
    extra = [jnp.where((row == 1) & (lane == q), 1.0, ones) for q in (0, LANES - 1)]

    def remap(c, carry):
        for k in range(GROUP // PIECE):
            load(c * (GROUP // PIECE) + k).wait()
        for k in range(lines // 8):
            levels(pl.multiple_of(c * lines + 8 * k, 8))
        parts, targets = [], []
        for k in range(GROUP):
            b = c * GROUP + k
            x = blocks[pl.ds(pl.multiple_of(b * 8, 8), 8), :]
            x = jnp.concatenate([x, extra[k & 1]], axis=0).astype(BF16)
            tiles = jnp.concatenate([weights_ref[b, 0], weights_ref[b, 1]], axis=1)
            product = jnp.dot(x, tiles, preferred_element_type=F32)
            for t in (0, 1):
                half = product[:, LANES * t : LANES * t + LANES]
                parts.append(half)
                targets.append(owner_ref[t, b] * WINDOWS + window_ref[t, b])
                line_ref[pl.ds(t * block_count + b, 1), :] = half[9:10]
        for first in range(0, len(parts), ACCS):
            here = range(first, first + ACCS)
            olds = [accs[i - first][targets[i]] for i in here]
            for i, old in zip(here, olds):
                accs[i - first][targets[i]] = old + parts[i]
        return carry

    lax.fori_loop(0, steps, remap, 0)
    line_out = pltpu.make_async_copy(line_ref, line_hbm, in_sems.at[6 + QUARTERS])
    line_out.start()

    def gather(o, carry):
        sums = []
        for w in range(WINDOWS):
            total = accs[0][o * WINDOWS + w]
            for acc in accs[1:]:
                total = total + acc[o * WINDOWS + w]
            part_ref[o, w * 8 : w * 8 + 8, :] = total[0:8]
            sums.append(total[8:9])
        part_ref[o, 32:40, :] = jnp.concatenate(sums + [jnp.zeros((4, LANES), F32)], axis=0)
        return carry

    size = part_ref.shape[0] // QUARTERS
    for k in range(QUARTERS):
        lax.fori_loop(k * size, (k + 1) * size, gather, 0)
        spot = pl.ds(k * size, size)
        outs.append(pltpu.make_async_copy(part_ref.at[spot], part_hbm.at[spot], in_sems.at[5 + k]))
        outs[-1].start()
    for out in outs + [line_out]:
        out.wait()


def remap_inner(route, winds, fields, far, near, weights, owners):
    count = weights.shape[0]
    return pl.pallas_call(
        remap_kernel,
        out_shape=(
            pltpu.HBM((8, CS), F32),
            pltpu.HBM((owners, 40, LANES), F32),
            pltpu.HBM((2 * count, LANES), F32),
            pltpu.HBM((2, CS, CS), F32),
            pltpu.HBM((2, CS, CS), F32),
        ),
        in_specs=[hbm()] * 2 + [vmem()] * 2 + [hbm()] * 4 + [anywhere()] * 2 + [hbm()],
        out_specs=(vmem(),) + (hbm(),) * 4,
        scratch_shapes=[
            pltpu.VMEM((owners, 40, LANES), F32),
            pltpu.VMEM((count * 8, LANES), F32),
            pltpu.VMEM((2 * count, LANES), F32),
            pltpu.SMEM((2, count), jnp.int32),
            pltpu.SMEM((2, count), jnp.int32),
            pltpu.VMEM((CS, CS), F32),
            pltpu.VMEM((CS, CS), F32),
            pltpu.VMEM((CS, CS), F32),
            pltpu.VMEM((4, CS, CS), F32),
            pltpu.VMEM((2, CS, CS), F32),
            pltpu.VMEM((2, CS, CS), F32),
            pltpu.VMEM(weights.shape, BF16),
        ]
        + [pltpu.VMEM((owners * WINDOWS, 16, LANES), F32)] * ACCS
        + [
            pltpu.SemaphoreType.DMA((count // PIECE,)),
            pltpu.SemaphoreType.DMA((7 + QUARTERS,)),
            pltpu.SemaphoreType.DMA((2, 4)),
        ],
        compiler_params=params(48),
        cost_estimate=cost(10**15, 1 << 40),
        name="stencil_remap",
    )(
        *[in_hbm(x) for x in route],
        *[in_vmem(x) for x in winds],
        *[in_hbm(x) for x in fields],
        far,
        near,
        in_hbm(weights),
    )


def reverse_lanes(x):
    rows = x.shape[0]
    i = lax.broadcasted_iota(jnp.int32, (CS, CS), 0)
    j = lax.broadcasted_iota(jnp.int32, (CS, CS), 1)
    flip = jnp.where(i + j == CS - 1, 1.0, 0.0).astype(BF16)
    high = x.astype(BF16)
    rest = x - high.astype(F32)
    mid = rest.astype(BF16)
    low = (rest - mid.astype(F32)).astype(BF16)
    parts = jnp.dot(jnp.concatenate([high, mid, low], axis=0), flip, preferred_element_type=F32)
    return parts[0:rows] + parts[rows : 2 * rows] + parts[2 * rows : 3 * rows]


def fix_kernel(
    source_ref,
    turns_ref,
    owner_ref,
    window_ref,
    owners_ref,
    windows_ref,
    own_ref,
    scale_hbm,
    edges_any,
    part_hbm,
    line_hbm,
    weights_hbm,
    send_hbm,
    delta_ref,
    scale_ref,
    got,
    ends,
    line_ref,
    send_ref,
    sems,
):
    edge_copies, copies = [pltpu.make_async_copy(scale_hbm, scale_ref, sems.at[8])], []
    for s in range(4):
        e = source_ref[0, s]
        spot = edges_any.at[e >> 2, pl.ds(pl.multiple_of((e & 3) * 8, 8), 8)]
        edge_copies.append(pltpu.make_async_copy(spot, got.at[s], sems.at[s]))
    block_count = weights_hbm.shape[0]
    for k, at in enumerate((0, block_count - 2)):
        copies.append(
            pltpu.make_async_copy(
                weights_hbm.at[pl.ds(at, 2)], ends.at[pl.ds(2 * k, 2)], sems.at[4 + k]
            )
        )
    copies.append(pltpu.make_async_copy(line_hbm, line_ref, sems.at[6]))
    copies.append(pltpu.make_async_copy(part_hbm, send_ref, sems.at[7]))
    for copy in edge_copies + copies:
        copy.start()
    for copy in edge_copies:
        copy.wait()

    upper = lax.broadcasted_iota(jnp.int32, (8, CS), 0) < 4
    sign = jnp.where(upper, -1.0, 1.0)
    turned = []
    for s in range(4):
        k = turns_ref[0, s]
        cosine = jnp.where(k == 0, 1.0, 0.0) - jnp.where(k == 2, 1.0, 0.0)
        sine = jnp.where(k == 1, 1.0, 0.0) - jnp.where(k == 3, 1.0, 0.0)
        edge = got[s]
        turned.append(cosine * edge + sine * (sign * pltpu.roll(edge, 4, 0)))
    flipped = reverse_lanes(jnp.concatenate(turned, axis=0))
    deltas = []
    for s in range(4):
        odd = (turns_ref[0, s] & 1) == 1
        halo = jnp.where(odd, flipped[8 * s : 8 * s + 8], turned[s])
        other = pltpu.roll(halo, 4, 0)
        energy = 0.5 * (halo * halo + other * other)
        out = -1.0 if s in (0, 3) else 1.0
        half = scale_ref[s : s + 1, :]
        if s < 2:
            vort = out * half * jnp.where(upper, other, halo)
            kinetic = jnp.where(upper, -out * half * energy, 0.0)
        else:
            vort = out * half * jnp.where(upper, halo, other)
            kinetic = jnp.where(upper, 0.0, out * half * energy)
        across = pltpu.roll(own_ref[8 * s : 8 * s + 8, :], 4, 0)
        delta = kinetic - sign * vort * across
        deltas.append(delta)
        delta_ref[s] = delta

    cell = lax.broadcasted_iota(jnp.int32, (CS, block_count), 0)
    block = lax.broadcasted_iota(jnp.int32, (CS, block_count), 1)
    for copy in copies:
        copy.wait()
    blank = jnp.zeros((8, LANES), F32)
    products = []
    for k in range(4):
        line = deltas[2 + k // 2][:, LANES * (k & 1) : LANES * (k & 1) + LANES]
        x = jnp.concatenate([line, blank], axis=0).astype(BF16)
        tiles = jnp.concatenate([ends[k, 0], ends[k, 1]], axis=1)
        products.append(jnp.dot(x, tiles, preferred_element_type=F32))
    for k, b in enumerate((0, 1, block_count - 2, block_count - 1)):
        for t in (0, 1):
            rows = pl.ds(pl.multiple_of(window_ref[t, b] * 8, 8), 8)
            send_ref[owner_ref[t, b], rows, :] += products[k][0:8, LANES * t : LANES * t + LANES]
    values = sum(
        jnp.dot(
            deltas[s].astype(BF16),
            jnp.where(block == 2 * cell + s, 1.0, 0.0).astype(BF16),
            preferred_element_type=F32,
        )
        for s in (0, 1)
    )
    values = jnp.concatenate([values, values], axis=1)
    lines = line_ref[...].astype(BF16)
    targets = owners_ref[...] * WINDOWS + windows_ref[...]
    targets = jnp.concatenate([targets[0:1], targets[1:2]], axis=1)
    targets = jnp.broadcast_to(targets, values.shape)
    owners = send_ref.shape[0]
    wide = WIDE
    outs = []
    for o in range(0, owners, wide):
        rows = [
            jnp.where(targets == w, values, 0.0)
            for w in range(o * WINDOWS, (o + wide) * WINDOWS)
        ]
        columns = jnp.dot(
            jnp.concatenate(rows, axis=0).astype(BF16), lines, preferred_element_type=F32
        )
        for k in range(wide):
            send_ref[o + k, 0:32, :] += columns[32 * k : 32 * k + 32]
        spot = pl.ds(o, wide)
        sem = sems.at[9 + o // wide]
        outs.append(pltpu.make_async_copy(send_ref.at[spot], send_hbm.at[spot], sem))
        outs[-1].start()
    for out in outs:
        out.wait()


def fix_edges(source, turns, route, own, scale, part, line, edges, weights):
    return pl.pallas_call(
        fix_kernel,
        out_shape=(pltpu.HBM(part.shape, F32), jax.ShapeDtypeStruct((4, 8, CS), F32)),
        in_specs=[smem()] * 4 + [vmem()] * 3 + [hbm(), anywhere()] + [hbm()] * 3,
        out_specs=(hbm(), vmem()),
        scratch_shapes=[
            pltpu.VMEM((8, CS), F32),
            pltpu.VMEM((4, 8, CS), F32),
            pltpu.VMEM((4, 2, LANES, LANES), BF16),
            pltpu.VMEM(line.shape, F32),
            pltpu.VMEM(part.shape, F32),
            pltpu.SemaphoreType.DMA((9 + part.shape[0] // WIDE,)),
        ],
        compiler_params=params(10),
        cost_estimate=cost(2 * 1024 * 1024 * 128, 3 << 20),
        name="edge_fix",
    )(
        source,
        turns,
        *route,
        *route,
        own,
        in_hbm(scale),
        edges,
        in_hbm(part),
        in_hbm(line),
        in_hbm(weights),
    )


def place_kernel(
    u_hbm,
    v_hbm,
    step_x_hbm,
    step_y_hbm,
    coriolis_hbm,
    lift_hbm,
    far_hbm,
    near_hbm,
    delta_ref,
    out_hbm,
    u_ref,
    v_ref,
    step_x_ref,
    step_y_ref,
    coriolis_ref,
    lift_ref,
    far_ref,
    near_ref,
    out_ref,
    cols,
    sems,
    out_sems,
):
    loads = half_loads(
        (u_hbm, v_hbm, step_x_hbm, step_y_hbm, coriolis_hbm, lift_hbm, far_hbm, near_hbm),
        (u_ref, v_ref, step_x_ref, step_y_ref, coriolis_ref, lift_ref, far_ref, near_ref),
        sems,
    )
    for load in loads[0] + loads[1]:
        load.start()
    cols[...] = jnp.transpose(
        jnp.concatenate(
            [delta_ref[0], delta_ref[1], jnp.zeros((LANES - 16, CS), F32)], axis=0
        )
    )
    lane = lax.broadcasted_iota(jnp.int32, (CHUNK, CS), 1)

    def put(r0, r, value):
        rows = pl.ds(r0, CHUNK)
        sides = cols[rows, :]
        left = jnp.where(lane == 0, sides[:, r : r + 1], 0.0)
        right = jnp.where(lane == CS - 1, sides[:, 8 + r : 9 + r], 0.0)
        out_ref[r // 4, r % 4, rows, :] = value + (left + right)

    inner = stencil_step(u_ref, v_ref, lift_ref, step_x_ref, step_y_ref, coriolis_ref, put)
    terms = outer_terms(lax.rem(lax.axis_index("lev"), 2), lift_ref, far_ref, near_ref)

    def step(c, carry):
        inner(c, carry)
        rows = pl.ds(pl.multiple_of(c * CHUNK, CHUNK), CHUNK)
        for comp, level, value in terms(rows):
            out_ref[comp, level, rows, :] += value
        return carry

    first, second = pl.ds(0, SPLIT * CHUNK), pl.ds(SPLIT * CHUNK, CS - SPLIT * CHUNK)
    outs = [
        pltpu.make_async_copy(out_ref.at[:, :, rows], out_hbm.at[:, :, rows], out_sems.at[k])
        for k, rows in enumerate((first, second))
    ]
    ends = ((0, SPLIT, 0, 2), (SPLIT, CS // CHUNK, CS - 1, 3))
    for h, (start, stop, line, side) in enumerate(ends):
        for load in loads[h]:
            load.wait()
        lax.fori_loop(start, stop, step, 0)
        for comp in (0, 1):
            for level in range(4):
                r = comp * 4 + level
                out_ref[comp, level, line : line + 1, :] += delta_ref[side, r : r + 1, :]
        outs[h].start()
    for out in outs:
        out.wait()


def place(fields, delta):
    return pl.pallas_call(
        place_kernel,
        out_shape=pltpu.HBM((2, 4, CS, CS), F32),
        in_specs=[hbm()] * len(fields) + [vmem()],
        out_specs=hbm(),
        scratch_shapes=[pltpu.VMEM(x.shape, F32) for x in fields]
        + [
            pltpu.VMEM((2, 4, CS, CS), F32),
            pltpu.VMEM((CS, LANES), F32),
            pltpu.SemaphoreType.DMA((2, len(fields))),
            pltpu.SemaphoreType.DMA((2,)),
        ],
        compiler_params=params(14),
        cost_estimate=cost(1 << 20, 8 << 20),
        name="place",
    )(*[in_hbm(x) for x in fields], delta)


def finish_kernel(got_ref, out_ref):
    total = got_ref[0]
    for d in range(1, got_ref.shape[0]):
        total = total + got_ref[d]
    for w in range(WINDOWS):
        share = total[8 * w : 8 * w + 8] / jnp.maximum(total[32 + w : 33 + w], 1.0)
        out_ref[0, :, LANES * w : LANES * w + LANES] = share[0:4]
        out_ref[1, :, LANES * w : LANES * w + LANES] = share[4:8]


def finish(got):
    return pl.pallas_call(
        finish_kernel,
        out_shape=jax.ShapeDtypeStruct((2, 4, WINDOWS * LANES), F32),
        in_specs=[vmem()],
        out_specs=vmem(),
        compiler_params=params(4),
        cost_estimate=cost(1000, 1 << 20),
        name="finish",
    )(got)


def per_device(
    wind_u,
    wind_v,
    vertical,
    spacing_x,
    spacing_y,
    coriolis,
    edge_source,
    edge_turns,
    route_owner,
    route_window,
    remap_weights,
):
    owners = lax.axis_size("sub")
    groups = lax.axis_size("lev")
    fields = (wind_u, wind_v, spacing_x, spacing_y, coriolis)
    edges, own, far, near, *winds = take_edges(fields[:2], owners)
    odds = range(1, groups - 1, 2)
    far = lax.ppermute(far, "lev", [(i, i + 1) for i in odds] + [(i + 1, i) for i in odds])
    near = lax.ppermute(near, "lev", [(i, i ^ 1) for i in range(groups)])
    edges = lax.all_to_all(edges, "sub", split_axis=0, concat_axis=0, tiled=True)
    route = (route_owner.T, route_window.T)
    scale, part, line, far, near = remap_inner(
        route, winds, fields[2:] + (vertical,), far, near, remap_weights, owners
    )
    send, delta = fix_edges(
        edge_source, edge_turns, route, own, scale, part, line, edges, remap_weights
    )
    got = lax.all_to_all(send, "sub", split_axis=0, concat_axis=0, tiled=True)
    return place(fields + (vertical, far, near), delta), finish(in_vmem(got))


def solution(mesh):
    placed = (
        P("lev", "sub", None),
        P("lev", "sub", None),
        P("lev", "sub", None),
        P("sub", None),
        P("sub", None),
        P("sub", None),
        P("sub", None),
        P("sub", None),
        P("sub", None),
        P("sub", None),
        P("sub", None, None, None),
    )
    return jax.shard_map(
        per_device,
        mesh=mesh,
        in_specs=placed,
        out_specs=(P(None, "lev", "sub", None), P(None, "lev", "sub")),
        check_vma=False,
    )
```
